256 devices in a mesh: group: 16 (over z, core), member: 16 (over x, y).
Axes of the slice: x: 4, y: 4, z: 8, core: 2. Of those that a mesh axis runs over, the one named last changes fastest.
Arguments:
- embeddings: bfloat16 [32, 8192, 768], P('group', 'member')
- counts: int32 [32], replicated, may hold values from 1 to 8192, as said below
Outputs:
- best_cosine: float32 [32, 8192], P('group', 'member')
The draws below stay inside these ranges and needn't reach their ends.
Inputs may be any that keep to these rules, and one draw needn't show every extreme that they name: Cluster c holds rows 0 to counts[c] - 1 of its 8192 slots; the rest are padding; some cluster fills all 8192 slots and some cluster holds a single row.
All inputs are finite; a program needn't handle non-finite values.
Results may differ from the reference program's by a relative error of at most 0.0003.
Values may be sent and summed in bfloat16 or wider, within the bound.
A program may use at most 128 MiB of HBM per device.

```python
import jax
import jax.numpy as jnp
from jax import lax

D = 768
ROWS_CL = 8192
NCL = 32


def draw_embeddings(key, part):
    key = jax.random.fold_in(key, 11)
    keys = jax.random.split(key, 4)
    base = jax.random.normal(keys[0], (NCL, ROWS_CL, D), jnp.float32)
    partner = jax.random.randint(keys[1], (NCL, ROWS_CL), 0, ROWS_CL)
    copied = jnp.take_along_axis(base, partner[:, :, None], axis=1)
    weight = jax.random.uniform(keys[2], (NCL, ROWS_CL, 1), jnp.float32, 0.0, 0.95)
    rows = jnp.sqrt(1.0 - weight * weight) * base + weight * copied
    common = 0.5 * jax.random.normal(keys[3], (D,), jnp.float32)
    level = 1.0 + 2.0 * jnp.arange(NCL, dtype=jnp.float32) / (NCL - 1)
    rows = rows + level[:, None, None] * common
    return rows.astype(jnp.bfloat16)


def draw_counts(key, part):
    key = jax.random.fold_in(key, 5)
    keys = jax.random.split(key, 2)
    level = jax.random.randint(keys[0], (NCL,), 0, 4096)
    square = level * level // 4096
    sizes = 1 + square * ROWS_CL // 4096
    order = jax.random.permutation(keys[1], NCL)
    sizes = sizes.at[order[0]].set(ROWS_CL)
    sizes = sizes.at[order[1]].set(1)
    sizes = sizes.at[order[2]].set(2)
    return jnp.clip(sizes, 1, ROWS_CL).astype(jnp.int32)


def setup_inputs(seed: int = 0) -> dict:
    streams_of = jax.random.split(jax.random.key(seed), 3)
    return {
        "embeddings": draw_embeddings(jax.random.fold_in(streams_of[2], 71), 0),
        "counts": draw_counts(jax.random.fold_in(streams_of[2], 71), 0),
    }


def reference(embeddings, counts):
    ncl, rcl, width = embeddings.shape
    pos = jnp.arange(rcl, dtype=jnp.int32)
    valid = pos[None, :] < counts[:, None]
    total = jnp.einsum('cr,crd->d', valid.astype(jnp.float32), embeddings.astype(jnp.float32))
    mean = total / jnp.sum(counts).astype(jnp.float32)

    def one_cluster(args):
        rows, count = args
        centered = rows.astype(jnp.float32) - mean
        unit = (centered / jnp.sqrt(lax.optimization_barrier(jnp.sum(centered * centered, axis=1, keepdims=True)) + 1e-06)).astype(jnp.bfloat16)
        scores = jnp.dot(unit, unit.T, preferred_element_type=jnp.float32)
        usable = (pos[None, :] < count) & (pos[:, None] != pos[None, :])
        best = lax.optimization_barrier(jnp.max(jnp.where(usable, scores, -jnp.inf), axis=1))
        best = jnp.maximum(best, jnp.float32(-1.0))
        return jnp.where(pos < count, best, jnp.float32(-1.0))
    return lax.map(one_cluster, (embeddings, counts))
```

```python
import jax
import jax.numpy as jnp
from jax import lax
from jax.experimental import pallas as pl
from jax.experimental.pallas import tpu as pltpu
from jax.sharding import PartitionSpec as P

MESH = pl.DeviceIdType.MESH
F32 = jnp.float32
LOW = -4.0
HALF = 256
BLOCK = 512
D = 768


def kernel(
    counts_ref, emb_ref, out_ref,
    yraw, uraw, draw, yu, uu, du, m_y, m_u, c_u, c_d,
    mbx, mby, mbc, mbz, r_y, r_u, r_d, in_y, in_u, in_d,
    xs_sem, y_sem, f_sem, u_sem, d_sem,
    mxs, mxr, mys, myr, mcs, mcr, mzs, mzr,
    rs_sem, iy_sem, iu_sem, id_sem,
):
    g = lax.axis_index("group")
    m = lax.axis_index("member")
    z, k = g // 2, g % 2
    x, y = m // 4, m % 4
    up, down = (y + 1) % 4, (y + 3) % 4
    half_d = (k + y // 2) % 2

    def dev(zz, kk, xx, yy):
        return (2 * zz + kk, 4 * xx + yy)

    def remote(src, dst, ssem, rsem, device):
        return pltpu.make_async_remote_copy(
            src_ref=src, dst_ref=dst, send_sem=ssem, recv_sem=rsem,
            device_id=device, device_id_type=MESH,
        )

    def recv(ref, sem):
        remote(ref, ref, sem, sem, dev(z, 1 - k, x, y)).wait_recv()

    barrier = pltpu.get_barrier_semaphore()

    def greet_plane(i, c):
        other = (16 * k + m + 1 + i) % 32
        pl.semaphore_signal(
            barrier, inc=1, device_id=(2 * z + other // 16, other % 16), device_id_type=MESH
        )
        return c

    def greet_z(i, c):
        pl.semaphore_signal(
            barrier, inc=1, device_id=(2 * ((z + 1 + i) % 8) + k, m), device_id_type=MESH
        )
        return c

    lax.fori_loop(0, 31, greet_plane, 0)
    lax.fori_loop(0, 7, greet_z, 0)

    total = jnp.zeros((8, D), F32)
    for s in range(2):
        left = counts_ref[4 * z + 2 * k + s] - BLOCK * m

        def add_rows(i, acc, s=s, left=left):
            rows = emb_ref[s, pl.ds(pl.multiple_of(i * 64, 64), 64), :].astype(F32)
            at = lax.broadcasted_iota(jnp.int32, (64, D), 0) + i * 64
            rows = jnp.where(at < left, rows, 0.0)
            return acc + jnp.sum(rows.reshape(8, 8, D), axis=0)

        total = lax.fori_loop(0, BLOCK // 64, add_rows, total)
    mbx[x] = total

    pl.semaphore_wait(barrier, 38)

    s_odd = (x + 1) % 2
    s_even = x % 2
    j_odd = 2 * k + s_odd
    j_even = 2 * k + s_even
    p_odd = jnp.where((x + 4 - j_odd) % 4 == 1, 1, 2)
    here = j_even == x

    def send_odd(h):
        return remote(
            emb_ref.at[s_odd, pl.ds(h * HALF, HALF)], yraw.at[p_odd, h],
            xs_sem.at[0, h], y_sem.at[p_odd, h], dev(z, h, j_odd, y),
        )

    def send_even(h, p):
        return remote(
            emb_ref.at[s_even, pl.ds(h * HALF, HALF)], yraw.at[p, h],
            xs_sem.at[1, h], y_sem.at[p, h], dev(z, h, j_even, y),
        )

    for h in range(2):
        @pl.when(here & (k == h))
        def _(h=h):
            pltpu.make_async_copy(
                emb_ref.at[s_even, pl.ds(h * HALF, HALF)], yraw.at[0, h], y_sem.at[0, h]
            ).start()

        @pl.when(here & (k != h))
        def _(h=h):
            send_even(h, 0).start()

    def exchange(buf, size, mine, ssem, rsem, device):
        def go(i, c):
            to = (mine + 1 + i) % size
            remote(buf.at[mine], buf.at[mine], ssem.at[i], rsem.at[mine], device(to)).start()
            return c

        lax.fori_loop(0, size - 1, go, 0)

    def collect(buf, size, mine, ssem, rsem, device):
        def done(i, c):
            frm = (mine + 1 + i) % size
            copy = remote(buf.at[mine], buf.at[frm], ssem.at[i], rsem.at[frm], device(frm))
            copy.wait_recv()
            copy.wait_send()
            return c

        lax.fori_loop(0, size - 1, done, 0)
        acc = buf[0]
        for i in range(1, size):
            acc = acc + buf[i]
        return acc

    on_x = lambda i: dev(z, k, i, y)
    on_y = lambda i: dev(z, k, x, i)
    on_c = lambda i: dev(z, i, x, y)
    on_z = lambda i: dev(i, k, x, y)

    exchange(mbx, 4, x, mxs, mxr, on_x)
    for h in range(2):
        send_odd(h).start()

    def forwards(p):
        src = yraw.at[p, k]
        return (
            remote(src, uraw.at[p], f_sem.at[p, 0], u_sem.at[p], dev(z, k, x, down)),
            remote(src, draw.at[p], f_sem.at[p, 1], d_sem.at[p],
                   dev(z, (k + up // 2) % 2, x, up)),
            remote(src, yraw.at[p, k], f_sem.at[p, 2], y_sem.at[p, k], dev(z, 1 - k, x, y)),
        )

    def arrive(p):
        recv(yraw.at[p, k], y_sem.at[p, k])
        for copy in forwards(p):
            copy.start()

    arrive(0)
    mby[y] = collect(mbx, 4, x, mxs, mxr, on_x)
    exchange(mby, 4, y, mys, myr, on_y)
    mbc[k] = collect(mby, 4, y, mys, myr, on_y)
    exchange(mbc, 2, k, mcs, mcr, on_c)
    mbz[z] = collect(mbc, 2, k, mcs, mcr, on_c)
    exchange(mbz, 8, z, mzs, mzr, on_z)
    summed = collect(mbz, 8, z, mzs, mzr, on_z)
    rows_all = counts_ref[0]
    for i in range(1, 32):
        rows_all = rows_all + counts_ref[i]
    mean = jnp.sum(summed, axis=0, keepdims=True) / rows_all.astype(F32)

    arrive(1)
    arrive(2)
    for h in range(2):
        send_odd(h).wait_send()

        @pl.when(j_even != x)
        def _(h=h):
            send_even(h, 3).start()

    n_home = counts_ref[4 * z + x]

    def origin(p):
        d = p + jnp.where(p == 2, 1, 0) - jnp.where(p == 3, 1, 0)
        return (x + d) % 4

    def left_y(p):
        return n_home - BLOCK * (4 * origin(p) + y)

    def left_u(p):
        return n_home - BLOCK * (4 * origin(p) + up) - HALF * k

    def left_d(p):
        return n_home - BLOCK * (4 * origin(p) + down) - HALF * half_d

    def normalise(src, dst):
        def step(i, c):
            at = pl.ds(pl.multiple_of(i * 32, 32), 32)
            v = src[at, :].astype(F32) - mean
            q = jnp.sum(v * v, axis=1, keepdims=True)
            dst[at, :] = (v * lax.rsqrt(q + 1e-06)).astype(jnp.bfloat16)
            return c

        lax.fori_loop(0, HALF // 32, step, 0)

    def scores(a, b):
        return lax.dot_general(
            a, b, (((1,), (1,)), ((), ())), preferred_element_type=F32
        )

    def bias(left):
        at = lax.broadcasted_iota(jnp.int32, (1, HALF), 1)
        return jnp.where(at < left, 0.0, LOW)

    def fold_lanes(sc):
        return jnp.maximum(sc[:, :128], sc[:, 128:])

    def fold_rows(sc):
        return jnp.max(sc.reshape(sc.shape[0] // 8, 8, sc.shape[1]), axis=0)

    def mask_rows(sc, left):
        at = lax.broadcasted_iota(jnp.int32, sc.shape, 0)
        return jnp.where(at < left, sc, LOW)

    def y_block(p):
        return yu[p].reshape(BLOCK, D)

    def own_tile(pr, pc):
        sc = scores(y_block(pr), yu[pc, k]) + bias(left_y(pc) - HALF * k)
        row = lax.broadcasted_iota(jnp.int32, sc.shape, 0)
        col = lax.broadcasted_iota(jnp.int32, sc.shape, 1) + HALF * k
        col = col + jnp.where(pr == pc, 0, BLOCK)
        sc = jnp.where(row == col, LOW, sc)
        m_y[pr] = jnp.maximum(m_y[pr], fold_lanes(sc))

    def up_tile(py, pu):
        sc = scores(y_block(py), uu[pu])
        m_y[py] = jnp.maximum(m_y[py], fold_lanes(sc + bias(left_u(pu))))
        c_u[pu] = jnp.maximum(c_u[pu], fold_rows(mask_rows(sc, left_y(py))))

    def cross_tile(pu, pd):
        sc = scores(uu[pu], du[pd])
        m_u[pu] = jnp.maximum(m_u[pu], fold_lanes(sc + bias(left_d(pd))))
        c_d[pd] = jnp.maximum(c_d[pd], fold_rows(mask_rows(sc, left_u(pu))))

    def loop(n, body):
        def step(i, c):
            body(i)
            return c

        lax.fori_loop(0, n, step, 0)

    def ready_y(p):
        normalise(yraw.at[p, k], yu.at[p, k])
        recv(yraw.at[p, 1 - k], y_sem.at[p, 1 - k])
        normalise(yraw.at[p, 1 - k], yu.at[p, 1 - k])

    def ready_ud(p, n_y):
        recv(uraw.at[p], u_sem.at[p])
        normalise(uraw.at[p], uu.at[p])
        loop(n_y, lambda py: up_tile(py, p))
        recv(draw.at[p], d_sem.at[p])
        normalise(draw.at[p], du.at[p])
        loop(p + 1, lambda pu: cross_tile(pu, p))
        loop(p, lambda pd: cross_tile(p, pd))

    m_y[...] = jnp.full(m_y.shape, LOW, F32)
    m_u[...] = jnp.full(m_u.shape, LOW, F32)
    c_u[...] = jnp.full(c_u.shape, LOW, F32)
    c_d[...] = jnp.full(c_d.shape, LOW, F32)

    loop(3, ready_y)
    loop(9, lambda i: own_tile(i // 3, i % 3))
    loop(2, lambda p: ready_ud(p, 3))
    arrive(3)
    ready_y(3)
    loop(4, lambda p: own_tile(p, 3))
    loop(3, lambda p: own_tile(3, p))
    loop(2, lambda p: up_tile(3, p))
    loop(2, lambda p: ready_ud(2 + p, 4))

    def flat(v):
        return jnp.max(v.T, axis=0, keepdims=True)

    s_home = x % 2
    k_home = x // 2

    def result_copies(p):
        xx = origin(p)
        return (
            remote(r_y.at[p], in_y.at[s_home, k], rs_sem.at[p, 0], iy_sem.at[s_home, k],
                   dev(z, k_home, xx, y)),
            remote(r_u.at[p], in_u.at[s_home, k], rs_sem.at[p, 1], iu_sem.at[s_home, k],
                   dev(z, k_home, xx, up)),
            remote(r_d.at[p], in_d.at[s_home, half_d], rs_sem.at[p, 2],
                   id_sem.at[s_home, half_d], dev(z, k_home, xx, down)),
        )

    mine = k == k_home
    for p in range(4):
        r_u[p] = jnp.maximum(flat(m_u[p]), jnp.max(c_u[p], axis=0, keepdims=True))
        r_d[p] = jnp.max(c_d[p], axis=0, keepdims=True)
        r_y[p] = flat(m_y[p])
        copies = result_copies(p)
        copies[1].start()
        copies[2].start()
        if p == 0:
            @pl.when(mine)
            def _():
                pltpu.make_async_copy(
                    r_y.at[0], in_y.at[s_home, k], iy_sem.at[s_home, k]
                ).start()

            @pl.when(jnp.logical_not(mine))
            def _():
                result_copies(0)[0].start()
        else:
            copies[0].start()

    for s in range(2):
        for h in range(2):
            recv(in_y.at[s, h], iy_sem.at[s, h])
            recv(in_u.at[s, h], iu_sem.at[s, h])
            recv(in_d.at[s, h], id_sem.at[s, h])
        best = jnp.maximum(in_y[s, 0], in_y[s, 1])
        both = jnp.concatenate(
            [jnp.maximum(in_u[s, h], in_d[s, h]) for h in range(2)], axis=1
        )
        best = jnp.maximum(jnp.maximum(best, both), -1.0)
        at = lax.broadcasted_iota(jnp.int32, (1, BLOCK), 1) + BLOCK * m
        n = counts_ref[4 * z + 2 * k + s]
        out_ref[s : s + 1, :] = jnp.where(at < n, best, -1.0)

    for h in range(2):
        @pl.when(here & (k != h))
        def _(h=h):
            send_even(h, 0).wait_send()

        @pl.when(j_even != x)
        def _(h=h):
            send_even(h, 3).wait_send()

    def finish(p):
        for copy in forwards(p):
            copy.wait_send()
        copies = result_copies(p)
        copies[1].wait_send()
        copies[2].wait_send()

        @pl.when((p > 0) | jnp.logical_not(mine))
        def _():
            result_copies(p)[0].wait_send()

    loop(4, finish)


def shards(embeddings, counts):
    dma = pltpu.SemaphoreType.DMA
    bf = jnp.bfloat16
    return pl.pallas_call(
        kernel,
        out_shape=jax.ShapeDtypeStruct((2, BLOCK), F32),
        in_specs=[
            pl.BlockSpec(memory_space=pltpu.SMEM),
            pl.BlockSpec(memory_space=pltpu.VMEM),
        ],
        out_specs=pl.BlockSpec(memory_space=pltpu.VMEM),
        scratch_shapes=[
            pltpu.VMEM((4, 2, HALF, D), bf),
            pltpu.VMEM((4, HALF, D), bf),
            pltpu.VMEM((4, HALF, D), bf),
            pltpu.VMEM((4, 2, HALF, D), bf),
            pltpu.VMEM((4, HALF, D), bf),
            pltpu.VMEM((4, HALF, D), bf),
            pltpu.VMEM((4, BLOCK, 128), F32),
            pltpu.VMEM((4, HALF, 128), F32),
            pltpu.VMEM((4, 8, HALF), F32),
            pltpu.VMEM((4, 8, HALF), F32),
            pltpu.VMEM((4, 8, D), F32),
            pltpu.VMEM((4, 8, D), F32),
            pltpu.VMEM((2, 8, D), F32),
            pltpu.VMEM((8, 8, D), F32),
            pltpu.VMEM((4, 1, BLOCK), F32),
            pltpu.VMEM((4, 1, HALF), F32),
            pltpu.VMEM((4, 1, HALF), F32),
            pltpu.VMEM((2, 2, 1, BLOCK), F32),
            pltpu.VMEM((2, 2, 1, HALF), F32),
            pltpu.VMEM((2, 2, 1, HALF), F32),
            dma((2, 2)), dma((4, 2)), dma((4, 3)), dma((4,)), dma((4,)),
            dma((3,)), dma((4,)), dma((3,)), dma((4,)),
            dma((1,)), dma((2,)), dma((7,)), dma((8,)),
            dma((4, 3)), dma((2, 2)), dma((2, 2)), dma((2, 2)),
        ],
        compiler_params=pltpu.CompilerParams(
            collective_id=0, has_side_effects=True, vmem_limit_bytes=48 * 1024 * 1024
        ),
        cost_estimate=pl.CostEstimate(
            flops=8 * 10**9, bytes_accessed=2 * 10**6, transcendentals=0
        ),
    )(counts, embeddings)


def solution(mesh):
    return jax.shard_map(
        shards,
        mesh=mesh,
        in_specs=(P("group", "member", None), P()),
        out_specs=P("group", "member"),
        check_vma=False,
    )
```

```python
import jax
import jax.numpy as jnp
from jax import lax
from jax.experimental import pallas as pl
from jax.experimental.pallas import tpu as pltpu
from jax.sharding import PartitionSpec as P

MESH = pl.DeviceIdType.MESH
F32 = jnp.float32
LOW = -4.0
HALF = 256
BLOCK = 512
D = 768


def kernel(
    counts_ref, emb_hbm, out_ref,
    emb_ref, relay, yraw, uraw, draw, yu, uu, du, m_y, m_u, c_u, c_d,
    mba, mbb, r_y, r_u, r_d, in_y, in_u, in_d,
    xs_sem, relay_s, relay_r, y_sem, f_sem, u_sem, d_sem,
    e_sem, as_sem, ar_sem, bs_sem, br_sem,
    rs_sem, iy_sem, iu_sem, id_sem,
):
    g = lax.axis_index("group")
    m = lax.axis_index("member")
    z, k = g // 2, g % 2
    x, y = m // 4, m % 4
    up, down = (y + 1) % 4, (y + 3) % 4
    half_d = (k + y // 2) % 2

    def dev(zz, kk, xx, yy):
        return (2 * zz + kk, 4 * xx + yy)

    def remote(src, dst, ssem, rsem, device):
        return pltpu.make_async_remote_copy(
            src_ref=src, dst_ref=dst, send_sem=ssem, recv_sem=rsem,
            device_id=device, device_id_type=MESH,
        )

    def recv(ref, sem):
        remote(ref, ref, sem, sem, dev(z, 1 - k, x, y)).wait_recv()

    load = pltpu.make_async_copy(emb_hbm, emb_ref, e_sem)
    load.start()
    barrier = pltpu.get_barrier_semaphore()

    def greet_plane(i, c):
        other = (16 * k + m + 1 + i) % 32
        pl.semaphore_signal(
            barrier, inc=1, device_id=(2 * z + other // 16, other % 16), device_id_type=MESH
        )
        return c

    def greet_z(i, c):
        zz = (z + 1 + i // 2) % 8
        pl.semaphore_signal(
            barrier, inc=1, device_id=(2 * zz + i % 2, m), device_id_type=MESH
        )
        return c

    lax.fori_loop(0, 31, greet_plane, 0)
    lax.fori_loop(0, 14, greet_z, 0)
    load.wait()

    total = jnp.zeros((8, D), F32)
    for s in range(2):
        left = counts_ref[4 * z + 2 * k + s] - BLOCK * m

        def add_rows(i, acc, s=s, left=left):
            rows = emb_ref[s, pl.ds(pl.multiple_of(i * 64, 64), 64), :].astype(F32)
            at = lax.broadcasted_iota(jnp.int32, (64, D), 0) + i * 64
            rows = jnp.where(at < left, rows, 0.0)
            return acc + jnp.sum(rows.reshape(8, 8, D), axis=0)

        total = lax.fori_loop(0, BLOCK // 64, add_rows, total)
    mba[m] = jnp.sum(total, axis=0, keepdims=True)

    pl.semaphore_wait(barrier, 45)

    s_odd = (x + 1) % 2
    s_even = x % 2
    j_odd = 2 * k + s_odd
    j_even = 2 * k + s_even
    p_odd = jnp.where((x + 4 - j_odd) % 4 == 1, 1, 2)
    here = j_even == x

    def send_odd(h):
        return remote(
            emb_ref.at[s_odd, pl.ds(h * HALF, HALF)], yraw.at[p_odd, h],
            xs_sem.at[0, h], y_sem.at[p_odd, h], dev(z, h, j_odd, y),
        )

    def send_own(h):
        return remote(
            emb_ref.at[s_even, pl.ds(h * HALF, HALF)], yraw.at[0, h],
            xs_sem.at[1, h], y_sem.at[0, h], dev(z, h, x, y),
        )

    def send_far(h):
        return remote(
            emb_ref.at[s_even, pl.ds(h * HALF, HALF)], relay,
            xs_sem.at[1, h], relay_r, dev(z, h, (x + 1 + 2 * h) % 4, y),
        )

    def pass_on():
        return remote(
            relay, yraw.at[3, k], relay_s, y_sem.at[3, k], dev(z, k, (x + 1 + 2 * k) % 4, y)
        )

    for h in range(2):
        @pl.when(here & (k == h))
        def _(h=h):
            pltpu.make_async_copy(
                emb_ref.at[s_even, pl.ds(h * HALF, HALF)], yraw.at[0, h], y_sem.at[0, h]
            ).start()

        @pl.when(here & (k != h))
        def _(h=h):
            send_own(h).start()

    def exchange(buf, mine, ssem, rsem, device):
        def go(i, c):
            remote(buf.at[mine], buf.at[mine], ssem, rsem, device((mine + 1 + i) % 16)).start()
            return c

        lax.fori_loop(0, 15, go, 0)

    def collect(buf, ssem, rsem):
        copy = remote(buf.at[:15], buf.at[:15], ssem, rsem, dev(z, 1 - k, x, y))
        copy.wait_recv()
        copy.wait_send()
        return jnp.sum(buf[...], axis=0)

    exchange(mba, m, as_sem, ar_sem, lambda i: (g, i))
    for h in range(2):
        send_odd(h).start()

    def forwards(p):
        src = yraw.at[p, k]
        return (
            remote(src, uraw.at[p], f_sem.at[p, 0], u_sem.at[p], dev(z, k, x, down)),
            remote(src, draw.at[p], f_sem.at[p, 1], d_sem.at[p],
                   dev(z, (k + up // 2) % 2, x, up)),
            remote(src, yraw.at[p, k], f_sem.at[p, 2], y_sem.at[p, k], dev(z, 1 - k, x, y)),
        )

    def arrive(p):
        recv(yraw.at[p, k], y_sem.at[p, k])
        for copy in forwards(p):
            copy.start()

    arrive(0)
    mbb[g] = collect(mba, as_sem, ar_sem)
    exchange(mbb, g, bs_sem, br_sem, lambda i: (i, m))
    arrive(1)
    for h in range(2):
        send_odd(h).wait_send()

        @pl.when(j_even != x)
        def _(h=h):
            send_far(h).start()

    summed = collect(mbb, bs_sem, br_sem)
    rows_all = counts_ref[0]
    for i in range(1, 32):
        rows_all = rows_all + counts_ref[i]
    mean = summed / rows_all.astype(F32)

    n_home = counts_ref[4 * z + x]

    def origin(p):
        d = p + jnp.where(p == 2, 1, 0) - jnp.where(p == 3, 1, 0)
        return (x + d) % 4

    def left_y(p):
        return n_home - BLOCK * (4 * origin(p) + y)

    def left_u(p):
        return n_home - BLOCK * (4 * origin(p) + up) - HALF * k

    def left_d(p):
        return n_home - BLOCK * (4 * origin(p) + down) - HALF * half_d

    def normalise(src, dst):
        def step(i, c):
            at = pl.ds(pl.multiple_of(i * 128, 128), 128)
            v = src[at, :].astype(F32) - mean
            q = jnp.sum(v * v, axis=1, keepdims=True)
            dst[at, :] = (v * lax.rsqrt(q + 1e-06)).astype(jnp.bfloat16)
            return c

        lax.fori_loop(0, HALF // 128, step, 0, unroll=2)

    def scores(a, b):
        return lax.dot_general(
            a, b, (((1,), (1,)), ((), ())), preferred_element_type=F32
        )

    def bias(left):
        at = lax.broadcasted_iota(jnp.int32, (1, HALF), 1)
        return jnp.where(at < left, 0.0, LOW)

    def fold_lanes(sc):
        return jnp.maximum(sc[:, :128], sc[:, 128:])

    def fold_rows(sc):
        return jnp.max(sc.reshape(sc.shape[0] // 8, 8, sc.shape[1]), axis=0)

    def mask_rows(sc, left):
        at = lax.broadcasted_iota(jnp.int32, sc.shape, 0)
        return jnp.where(at < left, sc, LOW)

    def y_block(p):
        return yu[p].reshape(BLOCK, D)

    def own_tile(pr, pc):
        sc = scores(y_block(pr), yu[pc, k]) + bias(left_y(pc) - HALF * k)
        row = lax.broadcasted_iota(jnp.int32, sc.shape, 0)
        col = lax.broadcasted_iota(jnp.int32, sc.shape, 1) + HALF * k
        col = col + jnp.where(pr == pc, 0, BLOCK)
        sc = jnp.where(row == col, LOW, sc)
        m_y[pr] = jnp.maximum(m_y[pr], fold_lanes(sc))

    def up_tile(py, pu):
        sc = scores(y_block(py), uu[pu])
        m_y[py] = jnp.maximum(m_y[py], fold_lanes(sc + bias(left_u(pu))))
        c_u[pu] = jnp.maximum(c_u[pu], fold_rows(mask_rows(sc, left_y(py))))

    def cross_tile(pu, pd):
        sc = scores(uu[pu], du[pd])
        m_u[pu] = jnp.maximum(m_u[pu], fold_lanes(sc + bias(left_d(pd))))
        c_d[pd] = jnp.maximum(c_d[pd], fold_rows(mask_rows(sc, left_u(pu))))

    def loop(n, body, unroll=1):
        def step(i, c):
            body(i)
            return c

        lax.fori_loop(0, n, step, 0, unroll=unroll)

    def ready_y(p):
        normalise(yraw.at[p, k], yu.at[p, k])
        recv(yraw.at[p, 1 - k], y_sem.at[p, 1 - k])
        normalise(yraw.at[p, 1 - k], yu.at[p, 1 - k])

    def ready_u(p, n_y):
        recv(uraw.at[p], u_sem.at[p])
        normalise(uraw.at[p], uu.at[p])
        loop(n_y, lambda py: up_tile(py, p), n_y)

    def ready_d(p):
        recv(draw.at[p], d_sem.at[p])
        normalise(draw.at[p], du.at[p])
        loop(p + 1, lambda pu: cross_tile(pu, p), p + 1)
        loop(p, lambda pd: cross_tile(p, pd), max(p, 1))

    m_y[...] = jnp.full(m_y.shape, LOW, F32)
    m_u[...] = jnp.full(m_u.shape, LOW, F32)
    c_u[...] = jnp.full(c_u.shape, LOW, F32)
    c_d[...] = jnp.full(c_d.shape, LOW, F32)

    loop(2, ready_y)
    loop(4, lambda i: own_tile(i // 2, i % 2), 4)
    arrive(2)
    recv(relay, relay_r)
    pass_on().start()
    ready_u(0, 2)
    ready_d(0)
    ready_y(2)
    loop(3, lambda p: own_tile(p, 2), 3)
    loop(2, lambda p: own_tile(2, p), 2)
    up_tile(2, 0)
    ready_u(1, 3)
    arrive(3)
    ready_d(1)
    ready_y(3)
    loop(4, lambda p: own_tile(p, 3), 4)
    loop(3, lambda p: own_tile(3, p), 3)
    loop(2, lambda p: up_tile(3, p), 2)
    ready_u(2, 4)
    ready_d(2)
    ready_u(3, 4)
    ready_d(3)

    def flat(v):
        return jnp.max(v.T, axis=0, keepdims=True)

    s_home = x % 2
    k_home = x // 2

    def result_copies(p):
        xx = origin(p)
        return (
            remote(r_y.at[p], in_y.at[s_home, k], rs_sem.at[p, 0], iy_sem.at[s_home, k],
                   dev(z, k_home, xx, y)),
            remote(r_u.at[p], in_u.at[s_home, k], rs_sem.at[p, 1], iu_sem.at[s_home, k],
                   dev(z, k_home, xx, up)),
            remote(r_d.at[p], in_d.at[s_home, half_d], rs_sem.at[p, 2],
                   id_sem.at[s_home, half_d], dev(z, k_home, xx, down)),
        )

    mine = k == k_home
    for p in range(4):
        r_u[p] = jnp.maximum(flat(m_u[p]), jnp.max(c_u[p], axis=0, keepdims=True))
        r_d[p] = jnp.max(c_d[p], axis=0, keepdims=True)
        r_y[p] = flat(m_y[p])
        copies = result_copies(p)
        copies[1].start()
        copies[2].start()
        if p == 0:
            @pl.when(mine)
            def _():
                pltpu.make_async_copy(
                    r_y.at[0], in_y.at[s_home, k], iy_sem.at[s_home, k]
                ).start()

            @pl.when(jnp.logical_not(mine))
            def _():
                result_copies(0)[0].start()
        else:
            copies[0].start()

    for s in range(2):
        for h in range(2):
            recv(in_y.at[s, h], iy_sem.at[s, h])
            recv(in_u.at[s, h], iu_sem.at[s, h])
            recv(in_d.at[s, h], id_sem.at[s, h])
        best = jnp.maximum(in_y[s, 0], in_y[s, 1])
        both = jnp.concatenate(
            [jnp.maximum(in_u[s, h], in_d[s, h]) for h in range(2)], axis=1
        )
        best = jnp.maximum(jnp.maximum(best, both), -1.0)
        at = lax.broadcasted_iota(jnp.int32, (1, BLOCK), 1) + BLOCK * m
        n = counts_ref[4 * z + 2 * k + s]
        out_ref[s : s + 1, :] = jnp.where(at < n, best, -1.0)

    pass_on().wait_send()
    for h in range(2):
        @pl.when(here & (k != h))
        def _(h=h):
            send_own(h).wait_send()

        @pl.when(j_even != x)
        def _(h=h):
            send_far(h).wait_send()

    def finish(p):
        for copy in forwards(p):
            copy.wait_send()
        copies = result_copies(p)
        copies[1].wait_send()
        copies[2].wait_send()

        @pl.when((p > 0) | jnp.logical_not(mine))
        def _():
            result_copies(p)[0].wait_send()

    loop(4, finish)


def shards(embeddings, counts):
    dma = pltpu.SemaphoreType.DMA
    bf = jnp.bfloat16
    return pl.pallas_call(
        kernel,
        out_shape=jax.ShapeDtypeStruct((2, BLOCK), F32),
        in_specs=[
            pl.BlockSpec(memory_space=pltpu.SMEM),
            pl.BlockSpec(memory_space=pl.ANY),
        ],
        out_specs=pl.BlockSpec(memory_space=pltpu.VMEM),
        scratch_shapes=[
            pltpu.VMEM((2, BLOCK, D), bf),
            pltpu.VMEM((HALF, D), bf),
            pltpu.VMEM((4, 2, HALF, D), bf),
            pltpu.VMEM((4, HALF, D), bf),
            pltpu.VMEM((4, HALF, D), bf),
            pltpu.VMEM((4, 2, HALF, D), bf),
            pltpu.VMEM((4, HALF, D), bf),
            pltpu.VMEM((4, HALF, D), bf),
            pltpu.VMEM((4, BLOCK, 128), F32),
            pltpu.VMEM((4, HALF, 128), F32),
            pltpu.VMEM((4, 8, HALF), F32),
            pltpu.VMEM((4, 8, HALF), F32),
            pltpu.VMEM((16, 1, D), F32),
            pltpu.VMEM((16, 1, D), F32),
            pltpu.VMEM((4, 1, BLOCK), F32),
            pltpu.VMEM((4, 1, HALF), F32),
            pltpu.VMEM((4, 1, HALF), F32),
            pltpu.VMEM((2, 2, 1, BLOCK), F32),
            pltpu.VMEM((2, 2, 1, HALF), F32),
            pltpu.VMEM((2, 2, 1, HALF), F32),
            dma((2, 2)), dma, dma, dma((4, 2)), dma((4, 3)), dma((4,)), dma((4,)),
            dma, dma, dma, dma, dma,
            dma((4, 3)), dma((2, 2)), dma((2, 2)), dma((2, 2)),
        ],
        compiler_params=pltpu.CompilerParams(
            collective_id=0, has_side_effects=True, vmem_limit_bytes=48 * 1024 * 1024
        ),
        cost_estimate=pl.CostEstimate(
            flops=8 * 10**9, bytes_accessed=2 * 10**6, transcendentals=0
        ),
    )(counts, embeddings)


def solution(mesh):
    return jax.shard_map(
        shards,
        mesh=mesh,
        in_specs=(P("group", "member", None), P()),
        out_specs=P("group", "member"),
        check_vma=False,
    )
```

```python
import jax
import jax.numpy as jnp
from jax import lax
from jax.experimental import pallas as pl
from jax.experimental.pallas import tpu as pltpu
from jax.sharding import PartitionSpec as P

MESH = pl.DeviceIdType.MESH
F32 = jnp.float32
LOW = -4.0
HALF = 256
BLOCK = 512
D = 768


def kernel(
    counts_ref, emb_hbm, out_ref,
    emb_ref, relay, yraw, uraw, draw, yu, uu, du, m_y, m_u, c_u, c_d,
    m_mine, m_row, m_col, m_pl, m_all, r_y, r_u, r_d, in_y, in_u, in_d,
    xs_sem, relay_s, relay_r, y_sem, f_sem, u_sem, d_sem,
    e_sem, ms_sem, mr_sem, cs_sem, cr_sem, ps_sem, pr_sem, ma_sem, ml_sem,
    rs_sem, iy_sem, iu_sem, id_sem,
):
    g = lax.axis_index("group")
    m = lax.axis_index("member")
    z, k = g // 2, g % 2
    x, y = m // 4, m % 4
    up, down = (y + 1) % 4, (y + 3) % 4
    half_d = (k + y // 2) % 2

    def dev(zz, kk, xx, yy):
        return (2 * zz + kk, 4 * xx + yy)

    def remote(src, dst, ssem, rsem, device):
        return pltpu.make_async_remote_copy(
            src_ref=src, dst_ref=dst, send_sem=ssem, recv_sem=rsem,
            device_id=device, device_id_type=MESH,
        )

    def recv(ref, sem):
        remote(ref, ref, sem, sem, dev(z, 1 - k, x, y)).wait_recv()

    load = pltpu.make_async_copy(emb_hbm, emb_ref, e_sem)
    load.start()
    barrier = pltpu.get_barrier_semaphore()

    chief = (x == 3) & (k == 0)

    def greet(device):
        pl.semaphore_signal(barrier, inc=1, device_id=device, device_id_type=MESH)

    greet(dev(z, 1 - k, x, y))
    for kk in range(2):
        for i in range(1, 4):
            greet(dev(z, kk, (x + i) % 4, y))
        greet(dev(z, kk, x, up))
        greet(dev(z, kk, x, down))

    @pl.when(chief)
    def _():
        greet(dev(z, k, x, (y + 2) % 4))
        for i in range(1, 8):
            greet(dev((z + i) % 8, k, x, y))

    load.wait()

    total = jnp.zeros((8, D), F32)
    for s in range(2):
        left = counts_ref[4 * z + 2 * k + s] - BLOCK * m

        def add_rows(i, acc, s=s, left=left):
            rows = emb_ref[s, pl.ds(pl.multiple_of(i * 64, 64), 64), :].astype(F32)
            at = lax.broadcasted_iota(jnp.int32, (64, D), 0) + i * 64
            rows = jnp.where(at < left, rows, 0.0)
            return acc + jnp.sum(rows.reshape(8, 8, D), axis=0)

        total = lax.fori_loop(0, BLOCK // 64, add_rows, total)
    m_mine[...] = jnp.sum(total, axis=0, keepdims=True)

    @pl.when(chief)
    def _():
        pl.semaphore_wait(barrier, 19)

    @pl.when(jnp.logical_not(chief))
    def _():
        pl.semaphore_wait(barrier, 11)


    row = 4 * k + x

    def to_chief():
        return remote(m_mine, m_row.at[row], ms_sem, mr_sem, dev(z, 0, 3, y))

    @pl.when(jnp.logical_not(chief))
    def _():
        to_chief().start()

    s_odd = (x + 1) % 2
    s_even = x % 2
    j_odd = 2 * k + s_odd
    j_even = 2 * k + s_even
    p_odd = jnp.where((x + 4 - j_odd) % 4 == 1, 1, 2)
    here = j_even == x

    def send_odd(h):
        return remote(
            emb_ref.at[s_odd, pl.ds(h * HALF, HALF)], yraw.at[p_odd, h],
            xs_sem.at[0, h], y_sem.at[p_odd, h], dev(z, h, j_odd, y),
        )

    def send_own(h):
        return remote(
            emb_ref.at[s_even, pl.ds(h * HALF, HALF)], yraw.at[0, h],
            xs_sem.at[1, h], y_sem.at[0, h], dev(z, h, x, y),
        )

    def send_far(h):
        return remote(
            emb_ref.at[s_even, pl.ds(h * HALF, HALF)], relay,
            xs_sem.at[1, h], relay_r, dev(z, h, (x + 1 + 2 * h) % 4, y),
        )

    def pass_on():
        return remote(
            relay, yraw.at[3, k], relay_s, y_sem.at[3, k], dev(z, k, (x + 1 + 2 * k) % 4, y)
        )

    for h in range(2):
        @pl.when(here & (k == h))
        def _(h=h):
            pltpu.make_async_copy(
                emb_ref.at[s_even, pl.ds(h * HALF, HALF)], yraw.at[0, h], y_sem.at[0, h]
            ).start()

        @pl.when(here & (k != h))
        def _(h=h):
            send_own(h).start()

    def send_mean(i):
        return remote(m_all, m_all, ma_sem, ml_sem, dev(z, i // 4, i % 4, y))

    def exchange(buf, size, mine, ssem, rsem, device):
        for i in range(1, size):
            to = (mine + i) % size
            remote(buf.at[mine], buf.at[mine], ssem, rsem, device(to)).start()

    def collect(buf, size, ssem, rsem):
        copy = remote(
            buf.at[: size - 1], buf.at[: size - 1], ssem, rsem, dev(z, 1 - k, x, y)
        )
        copy.wait_recv()
        copy.wait_send()
        return jnp.sum(buf[...], axis=0)

    for h in range(2):
        send_odd(h).start()

    def forwards(p):
        src = yraw.at[p, k]
        return (
            remote(src, uraw.at[p], f_sem.at[p, 0], u_sem.at[p], dev(z, k, x, down)),
            remote(src, draw.at[p], f_sem.at[p, 1], d_sem.at[p],
                   dev(z, (k + up // 2) % 2, x, up)),
            remote(src, yraw.at[p, k], f_sem.at[p, 2], y_sem.at[p, k], dev(z, 1 - k, x, y)),
        )

    def arrive(p):
        recv(yraw.at[p, k], y_sem.at[p, k])
        for copy in forwards(p):
            copy.start()

    @pl.when(chief)
    def _():
        m_row[3] = m_mine[...]
        recv(m_row.at[:7], mr_sem)
        m_col[y] = jnp.sum(m_row[...], axis=0)
        exchange(m_col, 4, y, cs_sem, cr_sem, lambda i: dev(z, k, x, i))

    arrive(0)

    @pl.when(chief)
    def _():
        m_pl[z] = collect(m_col, 4, cs_sem, cr_sem)
        exchange(m_pl, 8, z, ps_sem, pr_sem, lambda i: dev(i, k, x, y))
        m_all[...] = collect(m_pl, 8, ps_sem, pr_sem)
        for i in range(8):
            if i != 3:
                send_mean(i).start()

    arrive(1)
    for h in range(2):
        send_odd(h).wait_send()

        @pl.when(j_even != x)
        def _(h=h):
            send_far(h).start()

    arrive(2)
    recv(relay, relay_r)
    pass_on().start()

    @pl.when(jnp.logical_not(chief))
    def _():
        recv(m_all, ml_sem)

    rows_all = counts_ref[0]
    for i in range(1, 32):
        rows_all = rows_all + counts_ref[i]
    mean = m_all[...] / rows_all.astype(F32)

    n_home = counts_ref[4 * z + x]

    def origin(p):
        d = p + jnp.where(p == 2, 1, 0) - jnp.where(p == 3, 1, 0)
        return (x + d) % 4

    def left_y(p):
        return n_home - BLOCK * (4 * origin(p) + y)

    def left_u(p):
        return n_home - BLOCK * (4 * origin(p) + up) - HALF * k

    def left_d(p):
        return n_home - BLOCK * (4 * origin(p) + down) - HALF * half_d

    def normalise(src, dst):
        def step(i, c):
            at = pl.ds(pl.multiple_of(i * 128, 128), 128)
            v = src[at, :].astype(F32) - mean
            q = jnp.sum(v * v, axis=1, keepdims=True)
            dst[at, :] = (v * lax.rsqrt(q + 1e-06)).astype(jnp.bfloat16)
            return c

        lax.fori_loop(0, HALF // 128, step, 0, unroll=2)

    def scores(a, b):
        return lax.dot_general(
            a, b, (((1,), (1,)), ((), ())), preferred_element_type=F32
        )

    def bias(left):
        at = lax.broadcasted_iota(jnp.int32, (1, HALF), 1)
        return jnp.where(at < left, 0.0, LOW)

    def fold_lanes(sc):
        return jnp.maximum(sc[:, :128], sc[:, 128:])

    def fold_rows(sc):
        return jnp.max(sc.reshape(sc.shape[0] // 8, 8, sc.shape[1]), axis=0)

    def mask_rows(sc, left):
        at = lax.broadcasted_iota(jnp.int32, sc.shape, 0)
        return jnp.where(at < left, sc, LOW)

    def y_block(p):
        return yu[p].reshape(BLOCK, D)

    def own_tile(pr, pc):
        sc = scores(y_block(pr), yu[pc, k]) + bias(left_y(pc) - HALF * k)
        row = lax.broadcasted_iota(jnp.int32, sc.shape, 0)
        col = lax.broadcasted_iota(jnp.int32, sc.shape, 1) + HALF * k
        col = col + jnp.where(pr == pc, 0, BLOCK)
        sc = jnp.where(row == col, LOW, sc)
        m_y[pr] = jnp.maximum(m_y[pr], fold_lanes(sc))

    def up_tile(py, pu):
        sc = scores(y_block(py), uu[pu])
        m_y[py] = jnp.maximum(m_y[py], fold_lanes(sc + bias(left_u(pu))))
        c_u[pu] = jnp.maximum(c_u[pu], fold_rows(mask_rows(sc, left_y(py))))

    def cross_tile(pu, pd):
        sc = scores(uu[pu], du[pd])
        m_u[pu] = jnp.maximum(m_u[pu], fold_lanes(sc + bias(left_d(pd))))
        c_d[pd] = jnp.maximum(c_d[pd], fold_rows(mask_rows(sc, left_u(pu))))

    def loop(n, body, unroll=1):
        def step(i, c):
            body(i)
            return c

        lax.fori_loop(0, n, step, 0, unroll=unroll)

    def ready_y(p):
        normalise(yraw.at[p, k], yu.at[p, k])
        recv(yraw.at[p, 1 - k], y_sem.at[p, 1 - k])
        normalise(yraw.at[p, 1 - k], yu.at[p, 1 - k])

    def ready_u(p, n_y):
        recv(uraw.at[p], u_sem.at[p])
        normalise(uraw.at[p], uu.at[p])
        loop(n_y, lambda py: up_tile(py, p), n_y)

    def ready_d(p):
        recv(draw.at[p], d_sem.at[p])
        normalise(draw.at[p], du.at[p])
        loop(p + 1, lambda pu: cross_tile(pu, p), p + 1)
        loop(p, lambda pd: cross_tile(p, pd), max(p, 1))

    m_y[...] = jnp.full(m_y.shape, LOW, F32)
    m_u[...] = jnp.full(m_u.shape, LOW, F32)
    c_u[...] = jnp.full(c_u.shape, LOW, F32)
    c_d[...] = jnp.full(c_d.shape, LOW, F32)

    loop(2, ready_y)
    loop(4, lambda i: own_tile(i // 2, i % 2), 4)
    ready_u(0, 2)
    ready_d(0)
    ready_y(2)
    loop(3, lambda p: own_tile(p, 2), 3)
    loop(2, lambda p: own_tile(2, p), 2)
    up_tile(2, 0)
    ready_u(1, 3)
    arrive(3)
    ready_d(1)
    ready_y(3)
    loop(4, lambda p: own_tile(p, 3), 4)
    loop(3, lambda p: own_tile(3, p), 3)
    loop(2, lambda p: up_tile(3, p), 2)
    ready_u(2, 4)
    ready_d(2)
    ready_u(3, 4)
    ready_d(3)

    def flat(v):
        return jnp.max(v.T, axis=0, keepdims=True)

    s_home = x % 2
    k_home = x // 2

    def result_copies(p):
        xx = origin(p)
        return (
            remote(r_y.at[p], in_y.at[s_home, k], rs_sem.at[p, 0], iy_sem.at[s_home, k],
                   dev(z, k_home, xx, y)),
            remote(r_u.at[p], in_u.at[s_home, k], rs_sem.at[p, 1], iu_sem.at[s_home, k],
                   dev(z, k_home, xx, up)),
            remote(r_d.at[p], in_d.at[s_home, half_d], rs_sem.at[p, 2],
                   id_sem.at[s_home, half_d], dev(z, k_home, xx, down)),
        )

    mine = k == k_home
    for p in range(4):
        r_u[p] = jnp.maximum(flat(m_u[p]), jnp.max(c_u[p], axis=0, keepdims=True))
        r_d[p] = jnp.max(c_d[p], axis=0, keepdims=True)
        r_y[p] = flat(m_y[p])
        copies = result_copies(p)
        copies[1].start()
        copies[2].start()
        if p == 0:
            @pl.when(mine)
            def _():
                pltpu.make_async_copy(
                    r_y.at[0], in_y.at[s_home, k], iy_sem.at[s_home, k]
                ).start()

            @pl.when(jnp.logical_not(mine))
            def _():
                result_copies(0)[0].start()
        else:
            copies[0].start()

    for s in range(2):
        for h in range(2):
            recv(in_y.at[s, h], iy_sem.at[s, h])
            recv(in_u.at[s, h], iu_sem.at[s, h])
            recv(in_d.at[s, h], id_sem.at[s, h])
        best = jnp.maximum(in_y[s, 0], in_y[s, 1])
        both = jnp.concatenate(
            [jnp.maximum(in_u[s, h], in_d[s, h]) for h in range(2)], axis=1
        )
        best = jnp.maximum(jnp.maximum(best, both), -1.0)
        at = lax.broadcasted_iota(jnp.int32, (1, BLOCK), 1) + BLOCK * m
        n = counts_ref[4 * z + 2 * k + s]
        out_ref[s : s + 1, :] = jnp.where(at < n, best, -1.0)

    @pl.when(chief)
    def _():
        remote(m_row.at[:7], m_row.at[:7], ma_sem, ma_sem, dev(z, 1 - k, x, y)).wait_send()

    @pl.when(jnp.logical_not(chief))
    def _():
        to_chief().wait_send()

    pass_on().wait_send()
    for h in range(2):
        @pl.when(here & (k != h))
        def _(h=h):
            send_own(h).wait_send()

        @pl.when(j_even != x)
        def _(h=h):
            send_far(h).wait_send()

    def finish(p):
        for copy in forwards(p):
            copy.wait_send()
        copies = result_copies(p)
        copies[1].wait_send()
        copies[2].wait_send()

        @pl.when((p > 0) | jnp.logical_not(mine))
        def _():
            result_copies(p)[0].wait_send()

    loop(4, finish)


def shards(embeddings, counts):
    dma = pltpu.SemaphoreType.DMA
    bf = jnp.bfloat16
    return pl.pallas_call(
        kernel,
        out_shape=jax.ShapeDtypeStruct((2, BLOCK), F32),
        in_specs=[
            pl.BlockSpec(memory_space=pltpu.SMEM),
            pl.BlockSpec(memory_space=pl.ANY),
        ],
        out_specs=pl.BlockSpec(memory_space=pltpu.VMEM),
        scratch_shapes=[
            pltpu.VMEM((2, BLOCK, D), bf),
            pltpu.VMEM((HALF, D), bf),
            pltpu.VMEM((4, 2, HALF, D), bf),
            pltpu.VMEM((4, HALF, D), bf),
            pltpu.VMEM((4, HALF, D), bf),
            pltpu.VMEM((4, 2, HALF, D), bf),
            pltpu.VMEM((4, HALF, D), bf),
            pltpu.VMEM((4, HALF, D), bf),
            pltpu.VMEM((4, BLOCK, 128), F32),
            pltpu.VMEM((4, HALF, 128), F32),
            pltpu.VMEM((4, 8, HALF), F32),
            pltpu.VMEM((4, 8, HALF), F32),
            pltpu.VMEM((1, D), F32),
            pltpu.VMEM((8, 1, D), F32),
            pltpu.VMEM((4, 1, D), F32),
            pltpu.VMEM((8, 1, D), F32),
            pltpu.VMEM((1, D), F32),
            pltpu.VMEM((4, 1, BLOCK), F32),
            pltpu.VMEM((4, 1, HALF), F32),
            pltpu.VMEM((4, 1, HALF), F32),
            pltpu.VMEM((2, 2, 1, BLOCK), F32),
            pltpu.VMEM((2, 2, 1, HALF), F32),
            pltpu.VMEM((2, 2, 1, HALF), F32),
            dma((2, 2)), dma, dma, dma((4, 2)), dma((4, 3)), dma((4,)), dma((4,)),
            dma, dma, dma, dma, dma, dma, dma, dma, dma,
            dma((4, 3)), dma((2, 2)), dma((2, 2)), dma((2, 2)),
        ],
        compiler_params=pltpu.CompilerParams(
            collective_id=0, has_side_effects=True, vmem_limit_bytes=48 * 1024 * 1024
        ),
        cost_estimate=pl.CostEstimate(
            flops=8 * 10**9, bytes_accessed=2 * 10**6, transcendentals=0
        ),
    )(counts, embeddings)


def solution(mesh):
    return jax.shard_map(
        shards,
        mesh=mesh,
        in_specs=(P("group", "member", None), P()),
        out_specs=P("group", "member"),
        check_vma=False,
    )
```

```python
import jax
import jax.numpy as jnp
from jax import lax
from jax.experimental import pallas as pl
from jax.experimental.pallas import tpu as pltpu
from jax.sharding import PartitionSpec as P

MESH = pl.DeviceIdType.MESH
F32 = jnp.float32
LOW = -4.0
HALF = 256
BLOCK = 512
D = 768


def kernel(
    counts_hbm, emb_hbm, out_ref,
    counts_ref, emb_ref, relay, yraw, uraw, draw, yu, uu, du, m_y, m_u, c_u, c_d,
    m_mine, m_row, m_col, m_pl, m_all, r_y, r_u, r_d, in_y, in_u, in_d,
    xs_sem, relay_s, relay_r, y_sem, f_sem, u_sem, d_sem,
    e_sem, n_sem, ms_sem, mr_sem, cs_sem, cr_sem, ps_sem, pr_sem, ma_sem, ml_sem,
    rs_sem, iy_sem, iu_sem, id_sem,
):
    g = lax.axis_index("group")
    m = lax.axis_index("member")
    z, k = g // 2, g % 2
    x, y = m // 4, m % 4
    up, down = (y + 1) % 4, (y + 3) % 4
    half_d = (k + y // 2) % 2

    def dev(zz, kk, xx, yy):
        return (2 * zz + kk, 4 * xx + yy)

    def remote(src, dst, ssem, rsem, device):
        return pltpu.make_async_remote_copy(
            src_ref=src, dst_ref=dst, send_sem=ssem, recv_sem=rsem,
            device_id=device, device_id_type=MESH,
        )

    def recv(ref, sem):
        remote(ref, ref, sem, sem, dev(z, 1 - k, x, y)).wait_recv()

    load = pltpu.make_async_copy(emb_hbm, emb_ref, e_sem)
    load.start()
    sizes = pltpu.make_async_copy(counts_hbm, counts_ref, n_sem)
    sizes.start()
    barrier = pltpu.get_barrier_semaphore()

    chief = (x == 3) & (k == 0)

    def greet(device):
        pl.semaphore_signal(barrier, inc=1, device_id=device, device_id_type=MESH)

    greet(dev(z, 1 - k, x, y))
    for kk in range(2):
        for i in range(1, 4):
            greet(dev(z, kk, (x + i) % 4, y))
        greet(dev(z, kk, x, up))
        greet(dev(z, kk, x, down))

    @pl.when(chief)
    def _():
        greet(dev(z, k, x, (y + 2) % 4))
        for i in range(1, 8):
            greet(dev((z + i) % 8, k, x, y))

    sizes.wait()
    load.wait()

    total = jnp.zeros((8, D), F32)
    for s in range(2):
        left = counts_ref[4 * z + 2 * k + s] - BLOCK * m

        def add_rows(i, acc, s=s, left=left):
            rows = emb_ref[s, pl.ds(pl.multiple_of(i * 64, 64), 64), :].astype(F32)
            at = lax.broadcasted_iota(jnp.int32, (64, D), 0) + i * 64
            rows = jnp.where(at < left, rows, 0.0)
            return acc + jnp.sum(rows.reshape(8, 8, D), axis=0)

        total = lax.fori_loop(0, BLOCK // 64, add_rows, total)
    m_mine[...] = jnp.sum(total, axis=0, keepdims=True)

    @pl.when(chief)
    def _():
        pl.semaphore_wait(barrier, 19)

    @pl.when(jnp.logical_not(chief))
    def _():
        pl.semaphore_wait(barrier, 11)


    row = 4 * k + x

    def to_chief():
        return remote(m_mine, m_row.at[row], ms_sem, mr_sem, dev(z, 0, 3, y))

    @pl.when(jnp.logical_not(chief))
    def _():
        to_chief().start()

    s_odd = (x + 1) % 2
    s_even = x % 2
    j_odd = 2 * k + s_odd
    j_even = 2 * k + s_even
    p_odd = jnp.where((x + 4 - j_odd) % 4 == 1, 1, 2)
    here = j_even == x

    def send_odd(h):
        return remote(
            emb_ref.at[s_odd, pl.ds(h * HALF, HALF)], yraw.at[p_odd, h],
            xs_sem.at[0, h], y_sem.at[p_odd, h], dev(z, h, j_odd, y),
        )

    def send_own(h):
        return remote(
            emb_ref.at[s_even, pl.ds(h * HALF, HALF)], yraw.at[0, h],
            xs_sem.at[1, h], y_sem.at[0, h], dev(z, h, x, y),
        )

    def send_far(h):
        return remote(
            emb_ref.at[s_even, pl.ds(h * HALF, HALF)], relay,
            xs_sem.at[1, h], relay_r, dev(z, h, (x + 1 + 2 * h) % 4, y),
        )

    def pass_on():
        return remote(
            relay, yraw.at[3, k], relay_s, y_sem.at[3, k], dev(z, k, (x + 1 + 2 * k) % 4, y)
        )

    for h in range(2):
        @pl.when(here & (k == h))
        def _(h=h):
            pltpu.make_async_copy(
                emb_ref.at[s_even, pl.ds(h * HALF, HALF)], yraw.at[0, h], y_sem.at[0, h]
            ).start()

        @pl.when(here & (k != h))
        def _(h=h):
            send_own(h).start()

    def send_mean(i):
        return remote(m_all, m_all, ma_sem, ml_sem, dev(z, i // 4, i % 4, y))

    def exchange(buf, size, mine, ssem, rsem, device):
        for i in range(1, size):
            to = (mine + i) % size
            remote(buf.at[mine], buf.at[mine], ssem, rsem, device(to)).start()

    def collect(buf, size, ssem, rsem):
        copy = remote(
            buf.at[: size - 1], buf.at[: size - 1], ssem, rsem, dev(z, 1 - k, x, y)
        )
        copy.wait_recv()
        copy.wait_send()
        return jnp.sum(buf[...], axis=0)

    for h in range(2):
        send_odd(h).start()

    def forwards(p):
        src = yraw.at[p, k]
        return (
            remote(src, uraw.at[p], f_sem.at[p, 0], u_sem.at[p], dev(z, k, x, down)),
            remote(src, draw.at[p], f_sem.at[p, 1], d_sem.at[p],
                   dev(z, (k + up // 2) % 2, x, up)),
            remote(src, yraw.at[p, k], f_sem.at[p, 2], y_sem.at[p, k], dev(z, 1 - k, x, y)),
        )

    def arrive(p):
        recv(yraw.at[p, k], y_sem.at[p, k])
        for copy in forwards(p):
            copy.start()

    @pl.when(chief)
    def _():
        m_row[3] = m_mine[...]
        recv(m_row.at[:7], mr_sem)
        m_col[y] = jnp.sum(m_row[...], axis=0)
        exchange(m_col, 4, y, cs_sem, cr_sem, lambda i: dev(z, k, x, i))

    arrive(0)

    @pl.when(chief)
    def _():
        m_pl[z] = collect(m_col, 4, cs_sem, cr_sem)
        exchange(m_pl, 8, z, ps_sem, pr_sem, lambda i: dev(i, k, x, y))
        m_all[...] = collect(m_pl, 8, ps_sem, pr_sem)
        for i in range(8):
            if i != 3:
                send_mean(i).start()

    arrive(1)
    for h in range(2):
        send_odd(h).wait_send()

        @pl.when(j_even != x)
        def _(h=h):
            send_far(h).start()

    arrive(2)
    recv(relay, relay_r)
    pass_on().start()

    @pl.when(jnp.logical_not(chief))
    def _():
        recv(m_all, ml_sem)

    rows_all = counts_ref[0]
    for i in range(1, 32):
        rows_all = rows_all + counts_ref[i]
    mean = m_all[...] / rows_all.astype(F32)

    n_home = counts_ref[4 * z + x]

    def origin(p):
        d = p + jnp.where(p == 2, 1, 0) - jnp.where(p == 3, 1, 0)
        return (x + d) % 4

    def left_y(p):
        return n_home - BLOCK * (4 * origin(p) + y)

    def left_u(p):
        return n_home - BLOCK * (4 * origin(p) + up) - HALF * k

    def left_d(p):
        return n_home - BLOCK * (4 * origin(p) + down) - HALF * half_d

    def normalise(src, dst):
        def step(i, c):
            at = pl.ds(pl.multiple_of(i * 128, 128), 128)
            v = src[at, :].astype(F32) - mean
            q = jnp.sum(v * v, axis=1, keepdims=True)
            dst[at, :] = (v * lax.rsqrt(q + 1e-06)).astype(jnp.bfloat16)
            return c

        lax.fori_loop(0, HALF // 128, step, 0, unroll=2)

    def scores(a, b):
        return lax.dot_general(
            a, b, (((1,), (1,)), ((), ())), preferred_element_type=F32
        )

    def bias(left):
        at = lax.broadcasted_iota(jnp.int32, (1, HALF), 1)
        return jnp.where(at < left, 0.0, LOW)

    def fold_lanes(sc):
        return jnp.maximum(sc[:, :128], sc[:, 128:])

    def fold_rows(sc):
        return jnp.max(sc.reshape(sc.shape[0] // 8, 8, sc.shape[1]), axis=0)

    def mask_rows(sc, left):
        at = lax.broadcasted_iota(jnp.int32, sc.shape, 0)
        return jnp.where(at < left, sc, LOW)

    def y_block(p):
        return yu[p].reshape(BLOCK, D)

    def own_tile(pr, pc):
        sc = scores(y_block(pr), yu[pc, k]) + bias(left_y(pc) - HALF * k)
        row = lax.broadcasted_iota(jnp.int32, sc.shape, 0)
        col = lax.broadcasted_iota(jnp.int32, sc.shape, 1) + HALF * k
        col = col + jnp.where(pr == pc, 0, BLOCK)
        sc = jnp.where(row == col, LOW, sc)
        m_y[pr] = jnp.maximum(m_y[pr], fold_lanes(sc))

    def up_tile(py, pu):
        sc = scores(y_block(py), uu[pu])
        m_y[py] = jnp.maximum(m_y[py], fold_lanes(sc + bias(left_u(pu))))
        c_u[pu] = jnp.maximum(c_u[pu], fold_rows(mask_rows(sc, left_y(py))))

    def cross_tile(pu, pd):
        sc = scores(uu[pu], du[pd])
        m_u[pu] = jnp.maximum(m_u[pu], fold_lanes(sc + bias(left_d(pd))))
        c_d[pd] = jnp.maximum(c_d[pd], fold_rows(mask_rows(sc, left_u(pu))))

    def loop(n, body, unroll=1):
        def step(i, c):
            body(i)
            return c

        lax.fori_loop(0, n, step, 0, unroll=unroll)

    def ready_y(p):
        normalise(yraw.at[p, k], yu.at[p, k])
        recv(yraw.at[p, 1 - k], y_sem.at[p, 1 - k])
        normalise(yraw.at[p, 1 - k], yu.at[p, 1 - k])

    def ready_u(p, n_y):
        recv(uraw.at[p], u_sem.at[p])
        normalise(uraw.at[p], uu.at[p])
        loop(n_y, lambda py: up_tile(py, p), n_y)

    def ready_d(p):
        recv(draw.at[p], d_sem.at[p])
        normalise(draw.at[p], du.at[p])
        loop(p + 1, lambda pu: cross_tile(pu, p), p + 1)
        loop(p, lambda pd: cross_tile(p, pd), max(p, 1))

    m_y[...] = jnp.full(m_y.shape, LOW, F32)
    m_u[...] = jnp.full(m_u.shape, LOW, F32)
    c_u[...] = jnp.full(c_u.shape, LOW, F32)
    c_d[...] = jnp.full(c_d.shape, LOW, F32)

    loop(2, ready_y)
    loop(4, lambda i: own_tile(i // 2, i % 2), 4)
    ready_u(0, 2)
    ready_d(0)
    ready_y(2)
    loop(3, lambda p: own_tile(p, 2), 3)
    loop(2, lambda p: own_tile(2, p), 2)
    up_tile(2, 0)
    ready_u(1, 3)
    arrive(3)
    ready_d(1)
    ready_y(3)
    loop(4, lambda p: own_tile(p, 3), 4)
    loop(3, lambda p: own_tile(3, p), 3)
    loop(2, lambda p: up_tile(3, p), 2)
    ready_u(2, 4)
    ready_d(2)
    ready_u(3, 4)
    ready_d(3)

    def flat(v):
        return jnp.max(v.T, axis=0, keepdims=True)

    s_home = x % 2
    k_home = x // 2

    def result_copies(p):
        xx = origin(p)
        return (
            remote(r_y.at[p], in_y.at[s_home, k], rs_sem.at[p, 0], iy_sem.at[s_home, k],
                   dev(z, k_home, xx, y)),
            remote(r_u.at[p], in_u.at[s_home, k], rs_sem.at[p, 1], iu_sem.at[s_home, k],
                   dev(z, k_home, xx, up)),
            remote(r_d.at[p], in_d.at[s_home, half_d], rs_sem.at[p, 2],
                   id_sem.at[s_home, half_d], dev(z, k_home, xx, down)),
        )

    mine = k == k_home
    for p in range(4):
        r_u[p] = jnp.maximum(flat(m_u[p]), jnp.max(c_u[p], axis=0, keepdims=True))
        r_d[p] = jnp.max(c_d[p], axis=0, keepdims=True)
        r_y[p] = flat(m_y[p])
        copies = result_copies(p)
        copies[1].start()
        copies[2].start()
        if p == 0:
            @pl.when(mine)
            def _():
                pltpu.make_async_copy(
                    r_y.at[0], in_y.at[s_home, k], iy_sem.at[s_home, k]
                ).start()

            @pl.when(jnp.logical_not(mine))
            def _():
                result_copies(0)[0].start()
        else:
            copies[0].start()

    for s in range(2):
        for h in range(2):
            recv(in_y.at[s, h], iy_sem.at[s, h])
            recv(in_u.at[s, h], iu_sem.at[s, h])
            recv(in_d.at[s, h], id_sem.at[s, h])
        best = jnp.maximum(in_y[s, 0], in_y[s, 1])
        both = jnp.concatenate(
            [jnp.maximum(in_u[s, h], in_d[s, h]) for h in range(2)], axis=1
        )
        best = jnp.maximum(jnp.maximum(best, both), -1.0)
        at = lax.broadcasted_iota(jnp.int32, (1, BLOCK), 1) + BLOCK * m
        n = counts_ref[4 * z + 2 * k + s]
        out_ref[s : s + 1, :] = jnp.where(at < n, best, -1.0)

    @pl.when(chief)
    def _():
        remote(m_row.at[:7], m_row.at[:7], ma_sem, ma_sem, dev(z, 1 - k, x, y)).wait_send()

    @pl.when(jnp.logical_not(chief))
    def _():
        to_chief().wait_send()

    pass_on().wait_send()
    for h in range(2):
        @pl.when(here & (k != h))
        def _(h=h):
            send_own(h).wait_send()

        @pl.when(j_even != x)
        def _(h=h):
            send_far(h).wait_send()

    def finish(p):
        for copy in forwards(p):
            copy.wait_send()
        copies = result_copies(p)
        copies[1].wait_send()
        copies[2].wait_send()

        @pl.when((p > 0) | jnp.logical_not(mine))
        def _():
            result_copies(p)[0].wait_send()

    loop(4, finish)


def shards(embeddings, counts):
    dma = pltpu.SemaphoreType.DMA
    bf = jnp.bfloat16
    return pl.pallas_call(
        kernel,
        out_shape=jax.ShapeDtypeStruct((2, BLOCK), F32),
        in_specs=[
            pl.BlockSpec(memory_space=pl.ANY),
            pl.BlockSpec(memory_space=pl.ANY),
        ],
        out_specs=pl.BlockSpec(memory_space=pltpu.VMEM),
        scratch_shapes=[
            pltpu.SMEM((32,), jnp.int32),
            pltpu.VMEM((2, BLOCK, D), bf),
            pltpu.VMEM((HALF, D), bf),
            pltpu.VMEM((4, 2, HALF, D), bf),
            pltpu.VMEM((4, HALF, D), bf),
            pltpu.VMEM((4, HALF, D), bf),
            pltpu.VMEM((4, 2, HALF, D), bf),
            pltpu.VMEM((4, HALF, D), bf),
            pltpu.VMEM((4, HALF, D), bf),
            pltpu.VMEM((4, BLOCK, 128), F32),
            pltpu.VMEM((4, HALF, 128), F32),
            pltpu.VMEM((4, 8, HALF), F32),
            pltpu.VMEM((4, 8, HALF), F32),
            pltpu.VMEM((1, D), F32),
            pltpu.VMEM((8, 1, D), F32),
            pltpu.VMEM((4, 1, D), F32),
            pltpu.VMEM((8, 1, D), F32),
            pltpu.VMEM((1, D), F32),
            pltpu.VMEM((4, 1, BLOCK), F32),
            pltpu.VMEM((4, 1, HALF), F32),
            pltpu.VMEM((4, 1, HALF), F32),
            pltpu.VMEM((2, 2, 1, BLOCK), F32),
            pltpu.VMEM((2, 2, 1, HALF), F32),
            pltpu.VMEM((2, 2, 1, HALF), F32),
            dma((2, 2)), dma, dma, dma((4, 2)), dma((4, 3)), dma((4,)), dma((4,)),
            dma, dma, dma, dma, dma, dma, dma, dma, dma, dma,
            dma((4, 3)), dma((2, 2)), dma((2, 2)), dma((2, 2)),
        ],
        compiler_params=pltpu.CompilerParams(
            collective_id=0, has_side_effects=True, vmem_limit_bytes=64 * 1024 * 1024
        ),
        cost_estimate=pl.CostEstimate(
            flops=8 * 10**9, bytes_accessed=2 * 10**6, transcendentals=0
        ),
    )(counts, embeddings)


def solution(mesh):
    return jax.shard_map(
        shards,
        mesh=mesh,
        in_specs=(P("group", "member", None), P()),
        out_specs=P("group", "member"),
        check_vma=False,
    )
```

```python
import jax
import jax.numpy as jnp
from jax import lax
from jax.experimental import pallas as pl
from jax.experimental.pallas import tpu as pltpu
from jax.sharding import PartitionSpec as P

MESH = pl.DeviceIdType.MESH
F32 = jnp.float32
LOW = -4.0
HALF = 256
BLOCK = 512
D = 768


def kernel(
    counts_hbm, emb_hbm, out_ref,
    counts_ref, emb_ref, relay, yraw, uraw, draw, yu, uu, du, m_y, m_u, c_u, c_d,
    m_mine, m_row, m_col, m_pl, m_all, r_y, r_u, r_d, in_y, in_u, in_d,
    xs_sem, relay_s, relay_r, y_sem, f_sem, u_sem, d_sem,
    e_sem, n_sem, ms_sem, mr_sem, cs_sem, cr_sem, ps_sem, pr_sem, ma_sem, ml_sem,
    rs_sem, iy_sem, iu_sem, id_sem,
):
    g = lax.axis_index("group")
    m = lax.axis_index("member")
    z, k = g // 2, g % 2
    x, y = m // 4, m % 4
    up, down = (y + 1) % 4, (y + 3) % 4
    half_d = (k + y // 2) % 2

    def dev(zz, kk, xx, yy):
        return (2 * zz + kk, 4 * xx + yy)

    def remote(src, dst, ssem, rsem, device):
        return pltpu.make_async_remote_copy(
            src_ref=src, dst_ref=dst, send_sem=ssem, recv_sem=rsem,
            device_id=device, device_id_type=MESH,
        )

    def recv(ref, sem):
        remote(ref, ref, sem, sem, dev(z, 1 - k, x, y)).wait_recv()

    load = pltpu.make_async_copy(emb_hbm, emb_ref, e_sem)
    load.start()
    sizes = pltpu.make_async_copy(counts_hbm, counts_ref, n_sem)
    sizes.start()
    barrier = pltpu.get_barrier_semaphore()

    chief = (x == 3) & (k == 0)

    def greet(device):
        pl.semaphore_signal(barrier, inc=1, device_id=device, device_id_type=MESH)

    greet(dev(z, 1 - k, x, y))
    for kk in range(2):
        for i in range(1, 4):
            greet(dev(z, kk, (x + i) % 4, y))
        greet(dev(z, kk, x, up))
        greet(dev(z, kk, x, down))

    @pl.when(chief)
    def _():
        greet(dev(z, k, x, (y + 2) % 4))
        for i in range(1, 8):
            greet(dev((z + i) % 8, k, x, y))

    sizes.wait()
    load.wait()

    total = jnp.zeros((8, D), F32)
    for s in range(2):
        left = counts_ref[4 * z + 2 * k + s] - BLOCK * m

        def add_rows(i, acc, s=s, left=left):
            rows = emb_ref[s, pl.ds(pl.multiple_of(i * 64, 64), 64), :].astype(F32)
            at = lax.broadcasted_iota(jnp.int32, (64, D), 0) + i * 64
            rows = jnp.where(at < left, rows, 0.0)
            return acc + jnp.sum(rows.reshape(8, 8, D), axis=0)

        total = lax.fori_loop(0, BLOCK // 64, add_rows, total)
    m_mine[...] = jnp.sum(total, axis=0, keepdims=True)

    @pl.when(chief)
    def _():
        pl.semaphore_wait(barrier, 19)

    @pl.when(jnp.logical_not(chief))
    def _():
        pl.semaphore_wait(barrier, 11)


    row = 4 * k + x

    def to_chief():
        return remote(m_mine, m_row.at[row], ms_sem, mr_sem, dev(z, 0, 3, y))

    @pl.when(jnp.logical_not(chief))
    def _():
        to_chief().start()

    s_odd = (x + 1) % 2
    s_even = x % 2
    j_odd = 2 * k + s_odd
    j_even = 2 * k + s_even
    p_odd = jnp.where((x + 4 - j_odd) % 4 == 1, 1, 2)
    here = j_even == x

    def send_odd(h):
        return remote(
            emb_ref.at[s_odd, pl.ds(h * HALF, HALF)], yraw.at[p_odd, h],
            xs_sem.at[0, h], y_sem.at[p_odd, h], dev(z, h, j_odd, y),
        )

    def send_own(h):
        return remote(
            emb_ref.at[s_even, pl.ds(h * HALF, HALF)], yraw.at[0, h],
            xs_sem.at[1, h], y_sem.at[0, h], dev(z, h, x, y),
        )

    def send_far(h):
        return remote(
            emb_ref.at[s_even, pl.ds(h * HALF, HALF)], relay,
            xs_sem.at[1, h], relay_r, dev(z, h, (x + 1 + 2 * h) % 4, y),
        )

    def pass_on():
        return remote(
            relay, yraw.at[3, k], relay_s, y_sem.at[3, k], dev(z, k, (x + 1 + 2 * k) % 4, y)
        )

    for h in range(2):
        @pl.when(here & (k == h))
        def _(h=h):
            pltpu.make_async_copy(
                emb_ref.at[s_even, pl.ds(h * HALF, HALF)], yraw.at[0, h], y_sem.at[0, h]
            ).start()

        @pl.when(here & (k != h))
        def _(h=h):
            send_own(h).start()

    def send_mean(i):
        return remote(m_all, m_all, ma_sem, ml_sem, dev(z, i // 4, i % 4, y))

    def exchange(buf, size, mine, ssem, rsem, device):
        for i in range(1, size):
            to = (mine + i) % size
            remote(buf.at[mine], buf.at[mine], ssem, rsem, device(to)).start()

    def collect(buf, size, ssem, rsem):
        copy = remote(
            buf.at[: size - 1], buf.at[: size - 1], ssem, rsem, dev(z, 1 - k, x, y)
        )
        copy.wait_recv()
        copy.wait_send()
        return jnp.sum(buf[...], axis=0)

    for h in range(2):
        send_odd(h).start()

    @pl.when(j_even != x)
    def _():
        send_far(0).start()

    def forwards(p, src=None):
        src = yraw.at[p, k] if src is None else src
        return (
            remote(src, uraw.at[p], f_sem.at[p, 0], u_sem.at[p], dev(z, k, x, down)),
            remote(src, draw.at[p], f_sem.at[p, 1], d_sem.at[p],
                   dev(z, (k + up // 2) % 2, x, up)),
            remote(src, yraw.at[p, k], f_sem.at[p, 2], y_sem.at[p, k], dev(z, 1 - k, x, y)),
        )

    def arrive(p):
        recv(yraw.at[p, k], y_sem.at[p, k])
        for copy in forwards(p):
            copy.start()

    mine = here & (k == x // 2)

    @pl.when(mine)
    def _():
        for copy in forwards(0, emb_ref.at[s_even, pl.ds(pl.multiple_of(k * HALF, HALF), HALF)]):
            copy.start()

    @pl.when(chief)
    def _():
        m_row[3] = m_mine[...]
        recv(m_row.at[:7], mr_sem)
        m_col[y] = jnp.sum(m_row[...], axis=0)
        exchange(m_col, 4, y, cs_sem, cr_sem, lambda i: dev(z, k, x, i))

    @pl.when(jnp.logical_not(mine))
    def _():
        arrive(0)


    @pl.when(chief)
    def _():
        m_pl[z] = collect(m_col, 4, cs_sem, cr_sem)
        exchange(m_pl, 8, z, ps_sem, pr_sem, lambda i: dev(i, k, x, y))
        m_all[...] = collect(m_pl, 8, ps_sem, pr_sem)
        for i in range(8):
            if i != 3:
                send_mean(i).start()

    @pl.when(k == 0)
    def _():
        recv(relay, relay_r)
        pass_on().start()

    @pl.when(mine)
    def _():
        recv(yraw.at[0, k], y_sem.at[0, k])

    arrive(1)
    for h in range(2):
        send_odd(h).wait_send()

    @pl.when(j_even != x)
    def _():
        send_far(1).start()

    arrive(2)

    @pl.when(k == 1)
    def _():
        recv(relay, relay_r)
        pass_on().start()

    @pl.when(jnp.logical_not(chief))
    def _():
        recv(m_all, ml_sem)

    rows_all = counts_ref[0]
    for i in range(1, 32):
        rows_all = rows_all + counts_ref[i]
    mean = m_all[...] / rows_all.astype(F32)

    n_home = counts_ref[4 * z + x]

    def origin(p):
        d = p + jnp.where(p == 2, 1, 0) - jnp.where(p == 3, 1, 0)
        return (x + d) % 4

    def left_y(p):
        return n_home - BLOCK * (4 * origin(p) + y)

    def left_u(p):
        return n_home - BLOCK * (4 * origin(p) + up) - HALF * k

    def left_d(p):
        return n_home - BLOCK * (4 * origin(p) + down) - HALF * half_d

    def normalise(src, dst):
        def step(i, c):
            at = pl.ds(pl.multiple_of(i * 128, 128), 128)
            v = src[at, :].astype(F32) - mean
            q = jnp.sum(v * v, axis=1, keepdims=True)
            dst[at, :] = (v * lax.rsqrt(q + 1e-06)).astype(jnp.bfloat16)
            return c

        lax.fori_loop(0, HALF // 128, step, 0, unroll=2)

    def scores(a, b):
        return lax.dot_general(
            a, b, (((1,), (1,)), ((), ())), preferred_element_type=F32
        )

    def bias(left):
        at = lax.broadcasted_iota(jnp.int32, (1, HALF), 1)
        return jnp.where(at < left, 0.0, LOW)

    def fold_lanes(sc):
        return jnp.maximum(sc[:, :128], sc[:, 128:])

    def fold_rows(sc):
        return jnp.max(sc.reshape(sc.shape[0] // 8, 8, sc.shape[1]), axis=0)

    def mask_rows(sc, left):
        at = lax.broadcasted_iota(jnp.int32, sc.shape, 0)
        return jnp.where(at < left, sc, LOW)

    def y_block(p):
        return yu[p].reshape(BLOCK, D)

    def own_tile(pr, pc):
        sc = scores(y_block(pr), yu[pc, k]) + bias(left_y(pc) - HALF * k)
        row = lax.broadcasted_iota(jnp.int32, sc.shape, 0)
        col = lax.broadcasted_iota(jnp.int32, sc.shape, 1) + HALF * k
        col = col + jnp.where(pr == pc, 0, BLOCK)
        sc = jnp.where(row == col, LOW, sc)
        m_y[pr] = jnp.maximum(m_y[pr], fold_lanes(sc))

    def up_tile(py, pu):
        sc = scores(y_block(py), uu[pu])
        m_y[py] = jnp.maximum(m_y[py], fold_lanes(sc + bias(left_u(pu))))
        c_u[pu] = jnp.maximum(c_u[pu], fold_rows(mask_rows(sc, left_y(py))))

    def cross_tile(pu, pd):
        sc = scores(uu[pu], du[pd])
        m_u[pu] = jnp.maximum(m_u[pu], fold_lanes(sc + bias(left_d(pd))))
        c_d[pd] = jnp.maximum(c_d[pd], fold_rows(mask_rows(sc, left_u(pu))))

    def loop(n, body, unroll=1):
        def step(i, c):
            body(i)
            return c

        lax.fori_loop(0, n, step, 0, unroll=unroll)

    def ready_y(p):
        normalise(yraw.at[p, k], yu.at[p, k])
        recv(yraw.at[p, 1 - k], y_sem.at[p, 1 - k])
        normalise(yraw.at[p, 1 - k], yu.at[p, 1 - k])

    def ready_u(p, n_y):
        recv(uraw.at[p], u_sem.at[p])
        normalise(uraw.at[p], uu.at[p])
        loop(n_y, lambda py: up_tile(py, p), n_y)

    def ready_d(p):
        recv(draw.at[p], d_sem.at[p])
        normalise(draw.at[p], du.at[p])
        loop(p + 1, lambda pu: cross_tile(pu, p), p + 1)
        loop(p, lambda pd: cross_tile(p, pd), max(p, 1))

    m_y[...] = jnp.full(m_y.shape, LOW, F32)
    m_u[...] = jnp.full(m_u.shape, LOW, F32)
    c_u[...] = jnp.full(c_u.shape, LOW, F32)
    c_d[...] = jnp.full(c_d.shape, LOW, F32)

    loop(2, ready_y)
    loop(4, lambda i: own_tile(i // 2, i % 2), 4)
    ready_u(0, 2)
    ready_d(0)
    ready_y(2)
    loop(3, lambda p: own_tile(p, 2), 3)
    loop(2, lambda p: own_tile(2, p), 2)
    up_tile(2, 0)
    arrive(3)
    ready_u(1, 3)
    ready_d(1)
    ready_y(3)
    loop(4, lambda p: own_tile(p, 3), 4)
    loop(3, lambda p: own_tile(3, p), 3)
    loop(2, lambda p: up_tile(3, p), 2)
    ready_u(2, 4)
    ready_d(2)
    recv(uraw.at[3], u_sem.at[3])
    recv(draw.at[3], d_sem.at[3])
    normalise(uraw.at[3], uu.at[3])
    normalise(draw.at[3], du.at[3])
    for p in range(4):
        up_tile(p, 3)
    for p in range(4):
        cross_tile(p, 3)
    for p in range(3):
        cross_tile(3, p)

    def flat(v):
        return jnp.max(v.T, axis=0, keepdims=True)

    s_home = x % 2
    k_home = x // 2

    def result_copies(p):
        xx = origin(p)
        return (
            remote(r_y.at[p], in_y.at[s_home, k], rs_sem.at[p, 0], iy_sem.at[s_home, k],
                   dev(z, k_home, xx, y)),
            remote(r_u.at[p], in_u.at[s_home, k], rs_sem.at[p, 1], iu_sem.at[s_home, k],
                   dev(z, k_home, xx, up)),
            remote(r_d.at[p], in_d.at[s_home, half_d], rs_sem.at[p, 2],
                   id_sem.at[s_home, half_d], dev(z, k_home, xx, down)),
        )

    for p in range(4):
        r_u[p] = jnp.maximum(flat(m_u[p]), jnp.max(c_u[p], axis=0, keepdims=True))
        r_d[p] = jnp.max(c_d[p], axis=0, keepdims=True)
        r_y[p] = flat(m_y[p])
        copies = result_copies(p)
        copies[1].start()
        copies[2].start()
        if p == 0:
            @pl.when(mine)
            def _():
                pltpu.make_async_copy(
                    r_y.at[0], in_y.at[s_home, k], iy_sem.at[s_home, k]
                ).start()

            @pl.when(jnp.logical_not(mine))
            def _():
                result_copies(0)[0].start()
        else:
            copies[0].start()

    for s in range(2):
        for h in range(2):
            recv(in_y.at[s, h], iy_sem.at[s, h])
            recv(in_u.at[s, h], iu_sem.at[s, h])
            recv(in_d.at[s, h], id_sem.at[s, h])
        best = jnp.maximum(in_y[s, 0], in_y[s, 1])
        both = jnp.concatenate(
            [jnp.maximum(in_u[s, h], in_d[s, h]) for h in range(2)], axis=1
        )
        best = jnp.maximum(jnp.maximum(best, both), -1.0)
        at = lax.broadcasted_iota(jnp.int32, (1, BLOCK), 1) + BLOCK * m
        n = counts_ref[4 * z + 2 * k + s]
        out_ref[s : s + 1, :] = jnp.where(at < n, best, -1.0)

    @pl.when(chief)
    def _():
        remote(m_row.at[:7], m_row.at[:7], ma_sem, ma_sem, dev(z, 1 - k, x, y)).wait_send()

    @pl.when(jnp.logical_not(chief))
    def _():
        to_chief().wait_send()

    pass_on().wait_send()
    for h in range(2):
        @pl.when(here & (k != h))
        def _(h=h):
            send_own(h).wait_send()

        @pl.when(j_even != x)
        def _(h=h):
            send_far(h).wait_send()

    def finish(p):
        for copy in forwards(p):
            copy.wait_send()
        copies = result_copies(p)
        copies[1].wait_send()
        copies[2].wait_send()

        @pl.when((p > 0) | jnp.logical_not(mine))
        def _():
            result_copies(p)[0].wait_send()

    loop(4, finish)


def shards(embeddings, counts):
    dma = pltpu.SemaphoreType.DMA
    bf = jnp.bfloat16
    return pl.pallas_call(
        kernel,
        out_shape=jax.ShapeDtypeStruct((2, BLOCK), F32),
        in_specs=[
            pl.BlockSpec(memory_space=pl.ANY),
            pl.BlockSpec(memory_space=pl.ANY),
        ],
        out_specs=pl.BlockSpec(memory_space=pltpu.VMEM),
        scratch_shapes=[
            pltpu.SMEM((32,), jnp.int32),
            pltpu.VMEM((2, BLOCK, D), bf),
            pltpu.VMEM((HALF, D), bf),
            pltpu.VMEM((4, 2, HALF, D), bf),
            pltpu.VMEM((4, HALF, D), bf),
            pltpu.VMEM((4, HALF, D), bf),
            pltpu.VMEM((4, 2, HALF, D), bf),
            pltpu.VMEM((4, HALF, D), bf),
            pltpu.VMEM((4, HALF, D), bf),
            pltpu.VMEM((4, BLOCK, 128), F32),
            pltpu.VMEM((4, HALF, 128), F32),
            pltpu.VMEM((4, 8, HALF), F32),
            pltpu.VMEM((4, 8, HALF), F32),
            pltpu.VMEM((1, D), F32),
            pltpu.VMEM((8, 1, D), F32),
            pltpu.VMEM((4, 1, D), F32),
            pltpu.VMEM((8, 1, D), F32),
            pltpu.VMEM((1, D), F32),
            pltpu.VMEM((4, 1, BLOCK), F32),
            pltpu.VMEM((4, 1, HALF), F32),
            pltpu.VMEM((4, 1, HALF), F32),
            pltpu.VMEM((2, 2, 1, BLOCK), F32),
            pltpu.VMEM((2, 2, 1, HALF), F32),
            pltpu.VMEM((2, 2, 1, HALF), F32),
            dma((2, 2)), dma, dma, dma((4, 2)), dma((4, 3)), dma((4,)), dma((4,)),
            dma, dma, dma, dma, dma, dma, dma, dma, dma, dma,
            dma((4, 3)), dma((2, 2)), dma((2, 2)), dma((2, 2)),
        ],
        compiler_params=pltpu.CompilerParams(
            collective_id=0, has_side_effects=True, vmem_limit_bytes=64 * 1024 * 1024
        ),
        cost_estimate=pl.CostEstimate(
            flops=8 * 10**9, bytes_accessed=2 * 10**6, transcendentals=0
        ),
    )(counts, embeddings)


def solution(mesh):
    return jax.shard_map(
        shards,
        mesh=mesh,
        in_specs=(P("group", "member", None), P()),
        out_specs=P("group", "member"),
        check_vma=False,
    )
```

```python
import jax
import jax.numpy as jnp
from jax import lax
from jax.experimental import pallas as pl
from jax.experimental.pallas import tpu as pltpu
from jax.sharding import PartitionSpec as P

MESH = pl.DeviceIdType.MESH
F32 = jnp.float32
LOW = -4.0
HALF = 256
BLOCK = 512
D = 768


def kernel(
    counts_hbm, emb_hbm, out_ref,
    counts_ref, emb_ref, relay, yraw, uraw, draw, yu, uu, du, m_y, m_u, c_u, c_d,
    m_mine, m_row, m_col, m_pl, m_all, r_y, r_u, r_d, in_y, in_u, in_d,
    xs_sem, relay_s, relay_r, y_sem, f_sem, u_sem, d_sem,
    e_sem, n_sem, ms_sem, mr_sem, cs_sem, cr_sem, ps_sem, pr_sem, ma_sem, ml_sem,
    rs_sem, iy_sem, iu_sem, id_sem,
):
    g = lax.axis_index("group")
    m = lax.axis_index("member")
    z, k = g // 2, g % 2
    x, y = m // 4, m % 4
    up, down = (y + 1) % 4, (y + 3) % 4
    half_d = (k + y // 2) % 2

    def dev(zz, kk, xx, yy):
        return (2 * zz + kk, 4 * xx + yy)

    def remote(src, dst, ssem, rsem, device):
        return pltpu.make_async_remote_copy(
            src_ref=src, dst_ref=dst, send_sem=ssem, recv_sem=rsem,
            device_id=device, device_id_type=MESH,
        )

    def recv(ref, sem):
        remote(ref, ref, sem, sem, dev(z, 1 - k, x, y)).wait_recv()

    load = pltpu.make_async_copy(emb_hbm, emb_ref, e_sem)
    load.start()
    sizes = pltpu.make_async_copy(counts_hbm, counts_ref, n_sem)
    sizes.start()
    barrier = pltpu.get_barrier_semaphore()

    chief = (x == 3) & (k == 0)

    def greet(device):
        pl.semaphore_signal(barrier, inc=1, device_id=device, device_id_type=MESH)

    greet(dev(z, 1 - k, x, y))
    for kk in range(2):
        for i in range(1, 4):
            greet(dev(z, kk, (x + i) % 4, y))
        greet(dev(z, kk, x, up))
        greet(dev(z, kk, x, down))

    @pl.when(chief)
    def _():
        greet(dev(z, k, x, (y + 2) % 4))
        for i in range(1, 8):
            greet(dev((z + i) % 8, k, x, y))

    sizes.wait()
    load.wait()

    total = jnp.zeros((8, D), F32)
    for s in range(2):
        left = counts_ref[4 * z + 2 * k + s] - BLOCK * m

        def add_rows(i, acc, s=s, left=left):
            rows = emb_ref[s, pl.ds(pl.multiple_of(i * 64, 64), 64), :].astype(F32)
            at = lax.broadcasted_iota(jnp.int32, (64, D), 0) + i * 64
            rows = jnp.where(at < left, rows, 0.0)
            return acc + jnp.sum(rows.reshape(8, 8, D), axis=0)

        total = lax.fori_loop(0, BLOCK // 64, add_rows, total)
    m_mine[...] = jnp.sum(total, axis=0, keepdims=True)

    @pl.when(chief)
    def _():
        pl.semaphore_wait(barrier, 19)

    @pl.when(jnp.logical_not(chief))
    def _():
        pl.semaphore_wait(barrier, 11)


    row = 4 * k + x

    def to_chief():
        return remote(m_mine, m_row.at[row], ms_sem, mr_sem, dev(z, 0, 3, y))

    @pl.when(jnp.logical_not(chief))
    def _():
        to_chief().start()

    s_odd = (x + 1) % 2
    s_even = x % 2
    j_odd = 2 * k + s_odd
    j_even = 2 * k + s_even
    p_odd = jnp.where((x + 4 - j_odd) % 4 == 1, 1, 2)
    here = j_even == x

    def send_odd(h):
        return remote(
            emb_ref.at[s_odd, pl.ds(h * HALF, HALF)], yraw.at[p_odd, h],
            xs_sem.at[0, h], y_sem.at[p_odd, h], dev(z, h, j_odd, y),
        )

    def send_own(h):
        return remote(
            emb_ref.at[s_even, pl.ds(h * HALF, HALF)], yraw.at[0, h],
            xs_sem.at[1, h], y_sem.at[0, h], dev(z, h, x, y),
        )

    def send_far(h):
        return remote(
            emb_ref.at[s_even, pl.ds(h * HALF, HALF)], relay,
            xs_sem.at[1, h], relay_r, dev(z, h, (x + 1 + 2 * h) % 4, y),
        )

    def pass_on():
        return remote(
            relay, yraw.at[3, k], relay_s, y_sem.at[3, k], dev(z, k, (x + 1 + 2 * k) % 4, y)
        )

    for h in range(2):
        @pl.when(here & (k == h))
        def _(h=h):
            pltpu.make_async_copy(
                emb_ref.at[s_even, pl.ds(h * HALF, HALF)], yraw.at[0, h], y_sem.at[0, h]
            ).start()

        @pl.when(here & (k != h))
        def _(h=h):
            send_own(h).start()

    def send_mean(i):
        return remote(m_all, m_all, ma_sem, ml_sem, dev(z, i // 4, i % 4, y))

    def exchange(buf, size, mine, ssem, rsem, device):
        for i in range(1, size):
            to = (mine + i) % size
            remote(buf.at[mine], buf.at[mine], ssem, rsem, device(to)).start()

    def collect(buf, size, ssem, rsem):
        copy = remote(
            buf.at[: size - 1], buf.at[: size - 1], ssem, rsem, dev(z, 1 - k, x, y)
        )
        copy.wait_recv()
        copy.wait_send()
        return jnp.sum(buf[...], axis=0)

    for h in range(2):
        send_odd(h).start()

    @pl.when(j_even != x)
    def _():
        send_far(0).start()

    def forwards(p, src=None):
        src = yraw.at[p, k] if src is None else src
        return (
            remote(src, uraw.at[p], f_sem.at[p, 0], u_sem.at[p], dev(z, k, x, down)),
            remote(src, draw.at[p], f_sem.at[p, 1], d_sem.at[p],
                   dev(z, (k + up // 2) % 2, x, up)),
            remote(src, yraw.at[p, k], f_sem.at[p, 2], y_sem.at[p, k], dev(z, 1 - k, x, y)),
        )

    def arrive(p):
        recv(yraw.at[p, k], y_sem.at[p, k])
        for copy in forwards(p):
            copy.start()

    mine = here & (k == x // 2)

    @pl.when(mine)
    def _():
        for copy in forwards(0, emb_ref.at[s_even, pl.ds(pl.multiple_of(k * HALF, HALF), HALF)]):
            copy.start()

    @pl.when(chief)
    def _():
        m_row[3] = m_mine[...]
        recv(m_row.at[:7], mr_sem)
        m_col[y] = jnp.sum(m_row[...], axis=0)
        exchange(m_col, 4, y, cs_sem, cr_sem, lambda i: dev(z, k, x, i))

    @pl.when(jnp.logical_not(mine))
    def _():
        arrive(0)


    @pl.when(chief)
    def _():
        m_pl[z] = collect(m_col, 4, cs_sem, cr_sem)
        exchange(m_pl, 8, z, ps_sem, pr_sem, lambda i: dev(i, k, x, y))
        m_all[...] = collect(m_pl, 8, ps_sem, pr_sem)
        for i in range(8):
            if i != 3:
                send_mean(i).start()

    @pl.when(k == 0)
    def _():
        recv(relay, relay_r)
        pass_on().start()

    @pl.when(mine)
    def _():
        recv(yraw.at[0, k], y_sem.at[0, k])

    arrive(1)
    for h in range(2):
        send_odd(h).wait_send()

    @pl.when(j_even != x)
    def _():
        send_far(1).start()

    arrive(2)

    @pl.when(k == 1)
    def _():
        recv(relay, relay_r)
        pass_on().start()

    @pl.when(jnp.logical_not(chief))
    def _():
        recv(m_all, ml_sem)

    rows_all = counts_ref[0]
    for i in range(1, 32):
        rows_all = rows_all + counts_ref[i]
    mean = m_all[...] / rows_all.astype(F32)

    n_home = counts_ref[4 * z + x]

    def origin(p):
        d = p + jnp.where(p == 2, 1, 0) - jnp.where(p == 3, 1, 0)
        return (x + d) % 4

    def left_y(p):
        return n_home - BLOCK * (4 * origin(p) + y)

    def left_u(p):
        return n_home - BLOCK * (4 * origin(p) + up) - HALF * k

    def left_d(p):
        return n_home - BLOCK * (4 * origin(p) + down) - HALF * half_d

    def normalise(src, dst):
        def step(i, c):
            at = pl.ds(pl.multiple_of(i * 128, 128), 128)
            v = src[at, :].astype(F32) - mean
            q = jnp.sum(v * v, axis=1, keepdims=True)
            dst[at, :] = (v * lax.rsqrt(q + 1e-06)).astype(jnp.bfloat16)
            return c

        lax.fori_loop(0, HALF // 128, step, 0, unroll=2)

    def scores(a, b):
        return lax.dot_general(
            a, b, (((1,), (1,)), ((), ())), preferred_element_type=F32
        )

    def bias(left):
        at = lax.broadcasted_iota(jnp.int32, (1, HALF), 1)
        return jnp.where(at < left, 0.0, LOW)

    def fold_lanes(sc):
        return jnp.maximum(sc[:, :128], sc[:, 128:])

    def fold_rows(sc):
        return jnp.max(sc.reshape(sc.shape[0] // 8, 8, sc.shape[1]), axis=0)

    def mask_rows(sc, left):
        at = lax.broadcasted_iota(jnp.int32, sc.shape, 0)
        return jnp.where(at < left, sc, LOW)

    def y_block(p):
        return yu[p].reshape(BLOCK, D)

    def own_tile(pr, pc):
        sc = scores(y_block(pr), yu[pc, k]) + bias(left_y(pc) - HALF * k)
        row = lax.broadcasted_iota(jnp.int32, sc.shape, 0)
        col = lax.broadcasted_iota(jnp.int32, sc.shape, 1) + HALF * k
        col = col + jnp.where(pr == pc, 0, BLOCK)
        sc = jnp.where(row == col, LOW, sc)
        m_y[pr] = jnp.maximum(m_y[pr], fold_lanes(sc))

    def up_tile(py, pu):
        sc = scores(y_block(py), uu[pu])
        m_y[py] = jnp.maximum(m_y[py], fold_lanes(sc + bias(left_u(pu))))
        c_u[pu] = jnp.maximum(c_u[pu], fold_rows(mask_rows(sc, left_y(py))))

    def down_tile(pd):
        sc = scores(y_block(3), du[pd])
        m_y[3] = jnp.maximum(m_y[3], fold_lanes(sc + bias(left_d(pd))))
        c_d[pd] = jnp.maximum(c_d[pd], fold_rows(mask_rows(sc, left_y(3))))

    def cross_tile(pu, pd):
        sc = scores(uu[pu], du[pd])
        m_u[pu] = jnp.maximum(m_u[pu], fold_lanes(sc + bias(left_d(pd))))
        c_d[pd] = jnp.maximum(c_d[pd], fold_rows(mask_rows(sc, left_u(pu))))

    def loop(n, body, unroll=1):
        def step(i, c):
            body(i)
            return c

        lax.fori_loop(0, n, step, 0, unroll=unroll)

    def ready_y(p):
        normalise(yraw.at[p, k], yu.at[p, k])
        recv(yraw.at[p, 1 - k], y_sem.at[p, 1 - k])
        normalise(yraw.at[p, 1 - k], yu.at[p, 1 - k])

    def ready_u(p, n_y):
        recv(uraw.at[p], u_sem.at[p])
        normalise(uraw.at[p], uu.at[p])
        loop(n_y, lambda py: up_tile(py, p), n_y)

    def ready_d(p):
        recv(draw.at[p], d_sem.at[p])
        normalise(draw.at[p], du.at[p])
        loop(p + 1, lambda pu: cross_tile(pu, p), p + 1)
        loop(p, lambda pd: cross_tile(p, pd), max(p, 1))

    m_y[...] = jnp.full(m_y.shape, LOW, F32)
    m_u[...] = jnp.full(m_u.shape, LOW, F32)
    c_u[...] = jnp.full(c_u.shape, LOW, F32)
    c_d[...] = jnp.full(c_d.shape, LOW, F32)

    loop(2, ready_y)
    loop(4, lambda i: own_tile(i // 2, i % 2), 4)
    ready_u(0, 2)
    ready_d(0)
    ready_y(2)
    loop(3, lambda p: own_tile(p, 2), 3)
    loop(2, lambda p: own_tile(2, p), 2)
    up_tile(2, 0)
    arrive(3)
    ready_u(1, 3)
    ready_d(1)
    ready_y(3)
    loop(4, lambda p: own_tile(p, 3), 4)
    loop(3, lambda p: own_tile(3, p), 3)
    loop(2, lambda p: up_tile(3, p), 2)
    ready_u(2, 4)
    ready_d(2)
    for p in range(3):
        down_tile(p)

    def flat(v):
        return jnp.max(v.T, axis=0, keepdims=True)

    s_home = x % 2
    k_home = x // 2

    def result_copies(p):
        xx = origin(p)
        return (
            remote(r_y.at[p], in_y.at[s_home, k], rs_sem.at[p, 0], iy_sem.at[s_home, k],
                   dev(z, k_home, xx, y)),
            remote(r_u.at[p], in_u.at[s_home, k], rs_sem.at[p, 1], iu_sem.at[s_home, k],
                   dev(z, k_home, xx, up)),
            remote(r_d.at[p], in_d.at[s_home, half_d], rs_sem.at[p, 2],
                   id_sem.at[s_home, half_d], dev(z, k_home, xx, down)),
        )

    for p in range(3):
        r_y[p] = flat(m_y[p])
        if p == 0:
            @pl.when(mine)
            def _():
                pltpu.make_async_copy(
                    r_y.at[0], in_y.at[s_home, k], iy_sem.at[s_home, k]
                ).start()

            @pl.when(jnp.logical_not(mine))
            def _():
                result_copies(0)[0].start()
        else:
            result_copies(p)[0].start()

    recv(uraw.at[3], u_sem.at[3])
    recv(draw.at[3], d_sem.at[3])
    normalise(uraw.at[3], uu.at[3])
    normalise(draw.at[3], du.at[3])
    up_tile(3, 3)
    for p in range(4):
        cross_tile(p, 3)
    for p in range(3):
        cross_tile(3, p)
    r_y[3] = flat(m_y[3])
    result_copies(3)[0].start()
    for p in range(4):
        r_u[p] = jnp.maximum(flat(m_u[p]), jnp.max(c_u[p], axis=0, keepdims=True))
        r_d[p] = jnp.max(c_d[p], axis=0, keepdims=True)
        result_copies(p)[1].start()
        result_copies(p)[2].start()

    for s in range(2):
        for h in range(2):
            recv(in_y.at[s, h], iy_sem.at[s, h])
            recv(in_u.at[s, h], iu_sem.at[s, h])
            recv(in_d.at[s, h], id_sem.at[s, h])
        best = jnp.maximum(in_y[s, 0], in_y[s, 1])
        both = jnp.concatenate(
            [jnp.maximum(in_u[s, h], in_d[s, h]) for h in range(2)], axis=1
        )
        best = jnp.maximum(jnp.maximum(best, both), -1.0)
        at = lax.broadcasted_iota(jnp.int32, (1, BLOCK), 1) + BLOCK * m
        n = counts_ref[4 * z + 2 * k + s]
        out_ref[s : s + 1, :] = jnp.where(at < n, best, -1.0)

    @pl.when(chief)
    def _():
        remote(m_row.at[:7], m_row.at[:7], ma_sem, ma_sem, dev(z, 1 - k, x, y)).wait_send()

    @pl.when(jnp.logical_not(chief))
    def _():
        to_chief().wait_send()

    pass_on().wait_send()
    for h in range(2):
        @pl.when(here & (k != h))
        def _(h=h):
            send_own(h).wait_send()

        @pl.when(j_even != x)
        def _(h=h):
            send_far(h).wait_send()

    def finish(p):
        for copy in forwards(p):
            copy.wait_send()
        result_copies(p)[1].wait_send()
        result_copies(p)[2].wait_send()

        @pl.when((p > 0) | jnp.logical_not(mine))
        def _():
            result_copies(p)[0].wait_send()

    loop(4, finish)


def shards(embeddings, counts):
    dma = pltpu.SemaphoreType.DMA
    bf = jnp.bfloat16
    return pl.pallas_call(
        kernel,
        out_shape=jax.ShapeDtypeStruct((2, BLOCK), F32),
        in_specs=[
            pl.BlockSpec(memory_space=pl.ANY),
            pl.BlockSpec(memory_space=pl.ANY),
        ],
        out_specs=pl.BlockSpec(memory_space=pltpu.VMEM),
        scratch_shapes=[
            pltpu.SMEM((32,), jnp.int32),
            pltpu.VMEM((2, BLOCK, D), bf),
            pltpu.VMEM((HALF, D), bf),
            pltpu.VMEM((4, 2, HALF, D), bf),
            pltpu.VMEM((4, HALF, D), bf),
            pltpu.VMEM((4, HALF, D), bf),
            pltpu.VMEM((4, 2, HALF, D), bf),
            pltpu.VMEM((4, HALF, D), bf),
            pltpu.VMEM((4, HALF, D), bf),
            pltpu.VMEM((4, BLOCK, 128), F32),
            pltpu.VMEM((4, HALF, 128), F32),
            pltpu.VMEM((4, 8, HALF), F32),
            pltpu.VMEM((4, 8, HALF), F32),
            pltpu.VMEM((1, D), F32),
            pltpu.VMEM((8, 1, D), F32),
            pltpu.VMEM((4, 1, D), F32),
            pltpu.VMEM((8, 1, D), F32),
            pltpu.VMEM((1, D), F32),
            pltpu.VMEM((4, 1, BLOCK), F32),
            pltpu.VMEM((4, 1, HALF), F32),
            pltpu.VMEM((4, 1, HALF), F32),
            pltpu.VMEM((2, 2, 1, BLOCK), F32),
            pltpu.VMEM((2, 2, 1, HALF), F32),
            pltpu.VMEM((2, 2, 1, HALF), F32),
            dma((2, 2)), dma, dma, dma((4, 2)), dma((4, 3)), dma((4,)), dma((4,)),
            dma, dma, dma, dma, dma, dma, dma, dma, dma, dma,
            dma((4, 3)), dma((2, 2)), dma((2, 2)), dma((2, 2)),
        ],
        compiler_params=pltpu.CompilerParams(
            collective_id=0, has_side_effects=True, vmem_limit_bytes=64 * 1024 * 1024
        ),
        cost_estimate=pl.CostEstimate(
            flops=8 * 10**9, bytes_accessed=2 * 10**6, transcendentals=0
        ),
    )(counts, embeddings)


def solution(mesh):
    return jax.shard_map(
        shards,
        mesh=mesh,
        in_specs=(P("group", "member", None), P()),
        out_specs=P("group", "member"),
        check_vma=False,
    )
```

```python
import jax
import jax.numpy as jnp
from jax import lax
from jax.experimental import pallas as pl
from jax.experimental.pallas import tpu as pltpu
from jax.sharding import PartitionSpec as P

MESH = pl.DeviceIdType.MESH
F32 = jnp.float32
LOW = -4.0
HALF = 256
BLOCK = 512
D = 768


def kernel(
    counts_hbm, emb_hbm, out_ref,
    counts_ref, emb_ref, relay, yraw, uraw, draw, yu, uu, du, m_y, m_u, c_u, c_d,
    m_mine, m_row, m_col, m_pl, m_all, r_y, r_u, r_d, in_y, in_u, in_d,
    xs_sem, relay_s, relay_r, y_sem, f_sem, u_sem, d_sem,
    e_sem, n_sem, ms_sem, mr_sem, cs_sem, cr_sem, ps_sem, pr_sem, ma_sem, ml_sem,
    rs_sem, iy_sem, iu_sem, id_sem,
):
    g = lax.axis_index("group")
    m = lax.axis_index("member")
    z, k = g // 2, g % 2
    x, y = m // 4, m % 4
    up, down = (y + 1) % 4, (y + 3) % 4
    half_d = (k + y // 2) % 2

    def dev(zz, kk, xx, yy):
        return (2 * zz + kk, 4 * xx + yy)

    def remote(src, dst, ssem, rsem, device):
        return pltpu.make_async_remote_copy(
            src_ref=src, dst_ref=dst, send_sem=ssem, recv_sem=rsem,
            device_id=device, device_id_type=MESH,
        )

    def recv(ref, sem):
        remote(ref, ref, sem, sem, dev(z, 1 - k, x, y)).wait_recv()

    load = pltpu.make_async_copy(emb_hbm, emb_ref, e_sem)
    load.start()
    sizes = pltpu.make_async_copy(counts_hbm, counts_ref, n_sem)
    sizes.start()
    barrier = pltpu.get_barrier_semaphore()

    chief = (x == 3) & (k == 0)

    def greet(device):
        pl.semaphore_signal(barrier, inc=1, device_id=device, device_id_type=MESH)

    greet(dev(z, 1 - k, x, y))
    for kk in range(2):
        for i in range(1, 4):
            greet(dev(z, kk, (x + i) % 4, y))
        greet(dev(z, kk, x, up))
        greet(dev(z, kk, x, down))

    @pl.when(chief)
    def _():
        greet(dev(z, k, x, (y + 2) % 4))
        for i in range(1, 8):
            greet(dev((z + i) % 8, k, x, y))

    sizes.wait()
    load.wait()

    total = jnp.zeros((8, D), F32)
    for s in range(2):
        left = counts_ref[4 * z + 2 * k + s] - BLOCK * m

        def add_rows(i, acc, s=s, left=left):
            rows = emb_ref[s, pl.ds(pl.multiple_of(i * 64, 64), 64), :].astype(F32)
            at = lax.broadcasted_iota(jnp.int32, (64, D), 0) + i * 64
            rows = jnp.where(at < left, rows, 0.0)
            return acc + jnp.sum(rows.reshape(8, 8, D), axis=0)

        total = lax.fori_loop(0, BLOCK // 64, add_rows, total)
    m_mine[...] = jnp.sum(total, axis=0, keepdims=True)

    @pl.when(chief)
    def _():
        pl.semaphore_wait(barrier, 19)

    @pl.when(jnp.logical_not(chief))
    def _():
        pl.semaphore_wait(barrier, 11)


    row = 4 * k + x

    def to_chief():
        return remote(m_mine, m_row.at[row], ms_sem, mr_sem, dev(z, 0, 3, y))

    @pl.when(jnp.logical_not(chief))
    def _():
        to_chief().start()

    s_odd = (x + 1) % 2
    s_even = x % 2
    j_odd = 2 * k + s_odd
    j_even = 2 * k + s_even
    p_odd = jnp.where((x + 4 - j_odd) % 4 == 1, 1, 2)
    here = j_even == x

    def send_odd(h):
        return remote(
            emb_ref.at[s_odd, pl.ds(h * HALF, HALF)], yraw.at[p_odd, h],
            xs_sem.at[0, h], y_sem.at[p_odd, h], dev(z, h, j_odd, y),
        )

    def send_own(h):
        return remote(
            emb_ref.at[s_even, pl.ds(h * HALF, HALF)], yraw.at[0, h],
            xs_sem.at[1, h], y_sem.at[0, h], dev(z, h, x, y),
        )

    def send_far(h):
        return remote(
            emb_ref.at[s_even, pl.ds(h * HALF, HALF)], relay,
            xs_sem.at[1, h], relay_r, dev(z, h, (x + 1 + 2 * h) % 4, y),
        )

    def pass_on():
        return remote(
            relay, yraw.at[3, k], relay_s, y_sem.at[3, k], dev(z, k, (x + 1 + 2 * k) % 4, y)
        )

    for h in range(2):
        @pl.when(here & (k == h))
        def _(h=h):
            pltpu.make_async_copy(
                emb_ref.at[s_even, pl.ds(h * HALF, HALF)], yraw.at[0, h], y_sem.at[0, h]
            ).start()

        @pl.when(here & (k != h))
        def _(h=h):
            send_own(h).start()

    def send_mean(i):
        return remote(m_all, m_all, ma_sem, ml_sem, dev(z, i // 4, i % 4, y))

    def exchange(buf, size, mine, ssem, rsem, device):
        for i in range(1, size):
            to = (mine + i) % size
            remote(buf.at[mine], buf.at[mine], ssem, rsem, device(to)).start()

    def collect(buf, size, ssem, rsem):
        copy = remote(
            buf.at[: size - 1], buf.at[: size - 1], ssem, rsem, dev(z, 1 - k, x, y)
        )
        copy.wait_recv()
        copy.wait_send()
        return jnp.sum(buf[...], axis=0)

    for h in range(2):
        send_odd(h).start()

    @pl.when(j_even != x)
    def _():
        send_far(0).start()

    def forwards(p, src=None):
        src = yraw.at[p, k] if src is None else src
        return (
            remote(src, uraw.at[p], f_sem.at[p, 0], u_sem.at[p], dev(z, k, x, down)),
            remote(src, draw.at[p], f_sem.at[p, 1], d_sem.at[p],
                   dev(z, (k + up // 2) % 2, x, up)),
            remote(src, yraw.at[p, k], f_sem.at[p, 2], y_sem.at[p, k], dev(z, 1 - k, x, y)),
        )

    def arrive(p):
        recv(yraw.at[p, k], y_sem.at[p, k])
        for copy in forwards(p):
            copy.start()

    mine = here & (k == x // 2)

    @pl.when(mine)
    def _():
        for copy in forwards(0, emb_ref.at[s_even, pl.ds(pl.multiple_of(k * HALF, HALF), HALF)]):
            copy.start()

    @pl.when(chief)
    def _():
        m_row[3] = m_mine[...]
        recv(m_row.at[:7], mr_sem)
        m_col[y] = jnp.sum(m_row[...], axis=0)
        exchange(m_col, 4, y, cs_sem, cr_sem, lambda i: dev(z, k, x, i))

    @pl.when(jnp.logical_not(mine))
    def _():
        arrive(0)


    @pl.when(chief)
    def _():
        m_pl[z] = collect(m_col, 4, cs_sem, cr_sem)
        exchange(m_pl, 8, z, ps_sem, pr_sem, lambda i: dev(i, k, x, y))
        m_all[...] = collect(m_pl, 8, ps_sem, pr_sem)
        for i in range(8):
            if i != 3:
                send_mean(i).start()

    @pl.when(k == 0)
    def _():
        recv(relay, relay_r)
        pass_on().start()

    @pl.when(mine)
    def _():
        recv(yraw.at[0, k], y_sem.at[0, k])

    arrive(1)
    for h in range(2):
        send_odd(h).wait_send()

    @pl.when(j_even != x)
    def _():
        send_far(1).start()

    arrive(2)

    @pl.when(k == 1)
    def _():
        recv(relay, relay_r)
        pass_on().start()

    @pl.when(jnp.logical_not(chief))
    def _():
        recv(m_all, ml_sem)

    rows_all = counts_ref[0]
    for i in range(1, 32):
        rows_all = rows_all + counts_ref[i]
    mean = m_all[...] / rows_all.astype(F32)

    n_home = counts_ref[4 * z + x]

    def origin(p):
        d = p + jnp.where(p == 2, 1, 0) - jnp.where(p == 3, 1, 0)
        return (x + d) % 4

    def left_y(p):
        return n_home - BLOCK * (4 * origin(p) + y)

    def left_u(p):
        return n_home - BLOCK * (4 * origin(p) + up) - HALF * k

    def left_d(p):
        return n_home - BLOCK * (4 * origin(p) + down) - HALF * half_d

    def normalise(src, dst):
        def step(i, c):
            at = pl.ds(pl.multiple_of(i * 128, 128), 128)
            v = src[at, :].astype(F32) - mean
            q = jnp.sum(v * v, axis=1, keepdims=True)
            dst[at, :] = (v * lax.rsqrt(q + 1e-06)).astype(jnp.bfloat16)
            return c

        lax.fori_loop(0, HALF // 128, step, 0, unroll=2)

    def scores(a, b):
        return lax.dot_general(
            a, b, (((1,), (1,)), ((), ())), preferred_element_type=F32
        )

    def mask_cols(sc, left):
        at = lax.broadcasted_iota(jnp.int32, sc.shape, 1)
        return jnp.where(at < left, sc, LOW)

    def fold_lanes(sc):
        return jnp.maximum(sc[:, :128], sc[:, 128:])

    def fold_rows(sc):
        return jnp.max(sc.reshape(sc.shape[0] // 8, 8, sc.shape[1]), axis=0)

    def mask_rows(sc, left):
        at = lax.broadcasted_iota(jnp.int32, sc.shape, 0)
        return jnp.where(at < left, sc, LOW)

    def y_block(p):
        return yu[p].reshape(BLOCK, D)

    def own_tile(pr, pc):
        sc = mask_cols(scores(y_block(pr), yu[pc, k]), left_y(pc) - HALF * k)
        row = lax.broadcasted_iota(jnp.int32, sc.shape, 0)
        col = lax.broadcasted_iota(jnp.int32, sc.shape, 1) + HALF * k
        col = col + jnp.where(pr == pc, 0, BLOCK)
        sc = jnp.where(row == col, LOW, sc)
        m_y[pr] = jnp.maximum(m_y[pr], fold_lanes(sc))

    def up_tile(py, pu):
        sc = scores(y_block(py), uu[pu])
        m_y[py] = jnp.maximum(m_y[py], fold_lanes(mask_cols(sc, left_u(pu))))
        c_u[pu] = jnp.maximum(c_u[pu], fold_rows(mask_rows(sc, left_y(py))))

    def down_tile(pd):
        sc = scores(y_block(3), du[pd])
        m_y[3] = jnp.maximum(m_y[3], fold_lanes(mask_cols(sc, left_d(pd))))
        c_d[pd] = jnp.maximum(c_d[pd], fold_rows(mask_rows(sc, left_y(3))))

    def cross_tile(pu, pd):
        sc = scores(uu[pu], du[pd])
        m_u[pu] = jnp.maximum(m_u[pu], fold_lanes(mask_cols(sc, left_d(pd))))
        c_d[pd] = jnp.maximum(c_d[pd], fold_rows(mask_rows(sc, left_u(pu))))

    def loop(n, body, unroll=1):
        def step(i, c):
            body(i)
            return c

        lax.fori_loop(0, n, step, 0, unroll=unroll)

    def ready_y(p):
        normalise(yraw.at[p, k], yu.at[p, k])
        recv(yraw.at[p, 1 - k], y_sem.at[p, 1 - k])
        normalise(yraw.at[p, 1 - k], yu.at[p, 1 - k])

    def ready_u(p, n_y):
        recv(uraw.at[p], u_sem.at[p])
        normalise(uraw.at[p], uu.at[p])
        loop(n_y, lambda py: up_tile(py, p), n_y)

    def ready_d(p):
        recv(draw.at[p], d_sem.at[p])
        normalise(draw.at[p], du.at[p])
        loop(p + 1, lambda pu: cross_tile(pu, p), p + 1)
        loop(p, lambda pd: cross_tile(p, pd), max(p, 1))

    m_y[...] = jnp.full(m_y.shape, LOW, F32)
    m_u[...] = jnp.full(m_u.shape, LOW, F32)
    c_u[...] = jnp.full(c_u.shape, LOW, F32)
    c_d[...] = jnp.full(c_d.shape, LOW, F32)

    loop(2, ready_y)
    loop(4, lambda i: own_tile(i // 2, i % 2), 4)
    ready_u(0, 2)
    ready_d(0)
    ready_y(2)
    loop(3, lambda p: own_tile(p, 2), 3)
    loop(2, lambda p: own_tile(2, p), 2)
    up_tile(2, 0)
    arrive(3)
    ready_u(1, 3)
    ready_d(1)
    ready_y(3)
    loop(4, lambda p: own_tile(p, 3), 4)
    loop(3, lambda p: own_tile(3, p), 3)
    loop(2, lambda p: up_tile(3, p), 2)
    ready_u(2, 4)
    ready_d(2)
    for p in range(3):
        down_tile(p)

    def flat(v):
        return jnp.max(v.T, axis=0, keepdims=True)

    s_home = x % 2
    k_home = x // 2

    def result_copies(p):
        xx = origin(p)
        return (
            remote(r_y.at[p], in_y.at[s_home, k], rs_sem.at[p, 0], iy_sem.at[s_home, k],
                   dev(z, k_home, xx, y)),
            remote(r_u.at[p], in_u.at[s_home, k], rs_sem.at[p, 1], iu_sem.at[s_home, k],
                   dev(z, k_home, xx, up)),
            remote(r_d.at[p], in_d.at[s_home, half_d], rs_sem.at[p, 2],
                   id_sem.at[s_home, half_d], dev(z, k_home, xx, down)),
        )

    for p in range(3):
        r_y[p] = flat(m_y[p])
        if p == 0:
            @pl.when(mine)
            def _():
                pltpu.make_async_copy(
                    r_y.at[0], in_y.at[s_home, k], iy_sem.at[s_home, k]
                ).start()

            @pl.when(jnp.logical_not(mine))
            def _():
                result_copies(0)[0].start()
        else:
            result_copies(p)[0].start()

    recv(uraw.at[3], u_sem.at[3])
    recv(draw.at[3], d_sem.at[3])
    normalise(uraw.at[3], uu.at[3])
    normalise(draw.at[3], du.at[3])
    up_tile(3, 3)
    all_u = scores(uu[...].reshape(4 * HALF, D), du[3])
    for p in range(4):
        sc = all_u[p * HALF : (p + 1) * HALF]
        m_u[p] = jnp.maximum(m_u[p], fold_lanes(mask_cols(sc, left_d(3))))
        c_d[3] = jnp.maximum(c_d[3], fold_rows(mask_rows(sc, left_u(p))))
    for p in range(3):
        cross_tile(3, p)
    r_y[3] = flat(m_y[3])
    result_copies(3)[0].start()
    for p in range(4):
        r_u[p] = jnp.maximum(flat(m_u[p]), jnp.max(c_u[p], axis=0, keepdims=True))
        r_d[p] = jnp.max(c_d[p], axis=0, keepdims=True)
        result_copies(p)[1].start()
        result_copies(p)[2].start()

    for s in range(2):
        for h in range(2):
            recv(in_y.at[s, h], iy_sem.at[s, h])
            recv(in_u.at[s, h], iu_sem.at[s, h])
            recv(in_d.at[s, h], id_sem.at[s, h])
        best = jnp.maximum(in_y[s, 0], in_y[s, 1])
        both = jnp.concatenate(
            [jnp.maximum(in_u[s, h], in_d[s, h]) for h in range(2)], axis=1
        )
        best = jnp.maximum(jnp.maximum(best, both), -1.0)
        at = lax.broadcasted_iota(jnp.int32, (1, BLOCK), 1) + BLOCK * m
        n = counts_ref[4 * z + 2 * k + s]
        out_ref[s : s + 1, :] = jnp.where(at < n, best, -1.0)

    @pl.when(chief)
    def _():
        remote(m_row.at[:7], m_row.at[:7], ma_sem, ma_sem, dev(z, 1 - k, x, y)).wait_send()

    @pl.when(jnp.logical_not(chief))
    def _():
        to_chief().wait_send()

    pass_on().wait_send()
    for h in range(2):
        @pl.when(here & (k != h))
        def _(h=h):
            send_own(h).wait_send()

        @pl.when(j_even != x)
        def _(h=h):
            send_far(h).wait_send()

    def finish(p):
        for copy in forwards(p):
            copy.wait_send()
        result_copies(p)[1].wait_send()
        result_copies(p)[2].wait_send()

        @pl.when((p > 0) | jnp.logical_not(mine))
        def _():
            result_copies(p)[0].wait_send()

    loop(4, finish)


def shards(embeddings, counts):
    dma = pltpu.SemaphoreType.DMA
    bf = jnp.bfloat16
    return pl.pallas_call(
        kernel,
        out_shape=jax.ShapeDtypeStruct((2, BLOCK), F32),
        in_specs=[
            pl.BlockSpec(memory_space=pl.ANY),
            pl.BlockSpec(memory_space=pl.ANY),
        ],
        out_specs=pl.BlockSpec(memory_space=pltpu.VMEM),
        scratch_shapes=[
            pltpu.SMEM((32,), jnp.int32),
            pltpu.VMEM((2, BLOCK, D), bf),
            pltpu.VMEM((HALF, D), bf),
            pltpu.VMEM((4, 2, HALF, D), bf),
            pltpu.VMEM((4, HALF, D), bf),
            pltpu.VMEM((4, HALF, D), bf),
            pltpu.VMEM((4, 2, HALF, D), bf),
            pltpu.VMEM((4, HALF, D), bf),
            pltpu.VMEM((4, HALF, D), bf),
            pltpu.VMEM((4, BLOCK, 128), F32),
            pltpu.VMEM((4, HALF, 128), F32),
            pltpu.VMEM((4, 8, HALF), F32),
            pltpu.VMEM((4, 8, HALF), F32),
            pltpu.VMEM((1, D), F32),
            pltpu.VMEM((8, 1, D), F32),
            pltpu.VMEM((4, 1, D), F32),
            pltpu.VMEM((8, 1, D), F32),
            pltpu.VMEM((1, D), F32),
            pltpu.VMEM((4, 1, BLOCK), F32),
            pltpu.VMEM((4, 1, HALF), F32),
            pltpu.VMEM((4, 1, HALF), F32),
            pltpu.VMEM((2, 2, 1, BLOCK), F32),
            pltpu.VMEM((2, 2, 1, HALF), F32),
            pltpu.VMEM((2, 2, 1, HALF), F32),
            dma((2, 2)), dma, dma, dma((4, 2)), dma((4, 3)), dma((4,)), dma((4,)),
            dma, dma, dma, dma, dma, dma, dma, dma, dma, dma,
            dma((4, 3)), dma((2, 2)), dma((2, 2)), dma((2, 2)),
        ],
        compiler_params=pltpu.CompilerParams(
            collective_id=0, has_side_effects=True, vmem_limit_bytes=64 * 1024 * 1024
        ),
        cost_estimate=pl.CostEstimate(
            flops=8 * 10**9, bytes_accessed=2 * 10**6, transcendentals=0
        ),
    )(counts, embeddings)


def solution(mesh):
    return jax.shard_map(
        shards,
        mesh=mesh,
        in_specs=(P("group", "member", None), P()),
        out_specs=P("group", "member"),
        check_vma=False,
    )
```

```python
import jax
import jax.numpy as jnp
from jax import lax
from jax.experimental import pallas as pl
from jax.experimental.pallas import tpu as pltpu
from jax.sharding import PartitionSpec as P

MESH = pl.DeviceIdType.MESH
F32 = jnp.float32
LOW = -4.0
HALF = 256
BLOCK = 512
D = 768


def kernel(
    counts_hbm, emb_hbm, out_ref,
    counts_ref, emb_ref, relay, yraw, uraw, draw, yu, uu, du, m_y, m_u, c_u, c_d,
    m_mine, m_row, m_col, m_pl, m_all, r_y, r_u, r_d, in_y, in_u, in_d,
    xs_sem, relay_s, relay_r, y_sem, f_sem, u_sem, d_sem,
    e_sem, n_sem, ms_sem, mr_sem, cs_sem, cr_sem, ps_sem, pr_sem, ma_sem, ml_sem,
    rs_sem, iy_sem, iu_sem, id_sem,
):
    g = lax.axis_index("group")
    m = lax.axis_index("member")
    z, k = g // 2, g % 2
    x, y = m // 4, m % 4
    up, down = (y + 1) % 4, (y + 3) % 4
    half_d = (k + y // 2) % 2

    def dev(zz, kk, xx, yy):
        return (2 * zz + kk, 4 * xx + yy)

    def remote(src, dst, ssem, rsem, device):
        return pltpu.make_async_remote_copy(
            src_ref=src, dst_ref=dst, send_sem=ssem, recv_sem=rsem,
            device_id=device, device_id_type=MESH,
        )

    def recv(ref, sem):
        remote(ref, ref, sem, sem, dev(z, 1 - k, x, y)).wait_recv()

    load = pltpu.make_async_copy(emb_hbm, emb_ref, e_sem)
    load.start()
    sizes = pltpu.make_async_copy(counts_hbm, counts_ref, n_sem)
    sizes.start()
    barrier = pltpu.get_barrier_semaphore()

    chief = (x == 3) & (k == 0)

    def greet(device):
        pl.semaphore_signal(barrier, inc=1, device_id=device, device_id_type=MESH)

    greet(dev(z, 1 - k, x, y))
    for kk in range(2):
        for i in range(1, 4):
            greet(dev(z, kk, (x + i) % 4, y))
        greet(dev(z, kk, x, up))
        greet(dev(z, kk, x, down))

    @pl.when(chief)
    def _():
        greet(dev(z, k, x, (y + 2) % 4))
        for i in range(1, 8):
            greet(dev((z + i) % 8, k, x, y))

    sizes.wait()
    load.wait()

    total = jnp.zeros((8, D), F32)
    for s in range(2):
        left = counts_ref[4 * z + 2 * k + s] - BLOCK * m

        def add_rows(i, acc, s=s, left=left):
            rows = emb_ref[s, pl.ds(pl.multiple_of(i * 64, 64), 64), :].astype(F32)
            at = lax.broadcasted_iota(jnp.int32, (64, D), 0) + i * 64
            rows = jnp.where(at < left, rows, 0.0)
            return acc + jnp.sum(rows.reshape(8, 8, D), axis=0)

        total = lax.fori_loop(0, BLOCK // 64, add_rows, total)
    m_mine[...] = jnp.sum(total, axis=0, keepdims=True)

    @pl.when(chief)
    def _():
        pl.semaphore_wait(barrier, 19)

    @pl.when(jnp.logical_not(chief))
    def _():
        pl.semaphore_wait(barrier, 11)


    row = 4 * k + x

    def to_chief():
        return remote(m_mine, m_row.at[row], ms_sem, mr_sem, dev(z, 0, 3, y))

    @pl.when(jnp.logical_not(chief))
    def _():
        to_chief().start()

    s_odd = (x + 1) % 2
    s_even = x % 2
    j_odd = 2 * k + s_odd
    j_even = 2 * k + s_even
    p_odd = jnp.where((x + 4 - j_odd) % 4 == 1, 1, 2)
    here = j_even == x

    def send_odd(h):
        return remote(
            emb_ref.at[s_odd, pl.ds(h * HALF, HALF)], yraw.at[p_odd, h],
            xs_sem.at[0, h], y_sem.at[p_odd, h], dev(z, h, j_odd, y),
        )

    def send_own(h):
        return remote(
            emb_ref.at[s_even, pl.ds(h * HALF, HALF)], yraw.at[0, h],
            xs_sem.at[1, h], y_sem.at[0, h], dev(z, h, x, y),
        )

    def send_far(h):
        return remote(
            emb_ref.at[s_even, pl.ds(h * HALF, HALF)], relay,
            xs_sem.at[1, h], relay_r, dev(z, h, (x + 1 + 2 * h) % 4, y),
        )

    def pass_on():
        return remote(
            relay, yraw.at[3, k], relay_s, y_sem.at[3, k], dev(z, k, (x + 1 + 2 * k) % 4, y)
        )

    for h in range(2):
        @pl.when(here & (k == h))
        def _(h=h):
            pltpu.make_async_copy(
                emb_ref.at[s_even, pl.ds(h * HALF, HALF)], yraw.at[0, h], y_sem.at[0, h]
            ).start()

        @pl.when(here & (k != h))
        def _(h=h):
            send_own(h).start()

    def send_mean(i):
        return remote(m_all, m_all, ma_sem, ml_sem, dev(z, i // 4, i % 4, y))

    def exchange(buf, size, mine, ssem, rsem, device):
        for i in range(1, size):
            to = (mine + i) % size
            remote(buf.at[mine], buf.at[mine], ssem, rsem, device(to)).start()

    def collect(buf, size, ssem, rsem):
        copy = remote(
            buf.at[: size - 1], buf.at[: size - 1], ssem, rsem, dev(z, 1 - k, x, y)
        )
        copy.wait_recv()
        copy.wait_send()
        return jnp.sum(buf[...], axis=0)

    for h in range(2):
        send_odd(h).start()

    @pl.when(j_even != x)
    def _():
        send_far(0).start()

    def forwards(p, src=None):
        src = yraw.at[p, k] if src is None else src
        return (
            remote(src, uraw.at[p], f_sem.at[p, 0], u_sem.at[p], dev(z, k, x, down)),
            remote(src, draw.at[p], f_sem.at[p, 1], d_sem.at[p],
                   dev(z, (k + up // 2) % 2, x, up)),
            remote(src, yraw.at[p, k], f_sem.at[p, 2], y_sem.at[p, k], dev(z, 1 - k, x, y)),
        )

    def arrive(p):
        recv(yraw.at[p, k], y_sem.at[p, k])
        for copy in forwards(p):
            copy.start()

    mine = here & (k == x // 2)

    @pl.when(mine)
    def _():
        for copy in forwards(0, emb_ref.at[s_even, pl.ds(pl.multiple_of(k * HALF, HALF), HALF)]):
            copy.start()

    @pl.when(chief)
    def _():
        m_row[3] = m_mine[...]
        recv(m_row.at[:7], mr_sem)
        m_col[y] = jnp.sum(m_row[...], axis=0)
        exchange(m_col, 4, y, cs_sem, cr_sem, lambda i: dev(z, k, x, i))

    @pl.when(jnp.logical_not(mine))
    def _():
        arrive(0)


    @pl.when(chief)
    def _():
        m_pl[z] = collect(m_col, 4, cs_sem, cr_sem)
        exchange(m_pl, 8, z, ps_sem, pr_sem, lambda i: dev(i, k, x, y))
        m_all[...] = collect(m_pl, 8, ps_sem, pr_sem)
        for i in range(8):
            if i != 3:
                send_mean(i).start()

    @pl.when(k == 0)
    def _():
        recv(relay, relay_r)
        pass_on().start()

    @pl.when(mine)
    def _():
        recv(yraw.at[0, k], y_sem.at[0, k])

    arrive(1)
    arrive(2)
    for h in range(2):
        send_odd(h).wait_send()

    @pl.when(j_even != x)
    def _():
        send_far(1).start()


    @pl.when(k == 1)
    def _():
        recv(relay, relay_r)
        pass_on().start()

    @pl.when(jnp.logical_not(chief))
    def _():
        recv(m_all, ml_sem)

    rows_all = counts_ref[0]
    for i in range(1, 32):
        rows_all = rows_all + counts_ref[i]
    mean = m_all[...] / rows_all.astype(F32)

    n_home = counts_ref[4 * z + x]

    def origin(p):
        d = p + jnp.where(p == 2, 1, 0) - jnp.where(p == 3, 1, 0)
        return (x + d) % 4

    def left_y(p):
        return n_home - BLOCK * (4 * origin(p) + y)

    def left_u(p):
        return n_home - BLOCK * (4 * origin(p) + up) - HALF * k

    def left_d(p):
        return n_home - BLOCK * (4 * origin(p) + down) - HALF * half_d

    def normalise(src, dst):
        def step(i, c):
            at = pl.ds(pl.multiple_of(i * 128, 128), 128)
            v = src[at, :].astype(F32) - mean
            q = jnp.sum(v * v, axis=1, keepdims=True)
            dst[at, :] = (v * lax.rsqrt(q + 1e-06)).astype(jnp.bfloat16)
            return c

        lax.fori_loop(0, HALF // 128, step, 0, unroll=2)

    def scores(a, b):
        return lax.dot_general(
            a, b, (((1,), (1,)), ((), ())), preferred_element_type=F32
        )

    def mask_cols(sc, left):
        at = lax.broadcasted_iota(jnp.int32, sc.shape, 1)
        return jnp.where(at < left, sc, LOW)

    def fold_lanes(sc):
        return jnp.maximum(sc[:, :128], sc[:, 128:])

    def fold_rows(sc):
        return jnp.max(sc.reshape(sc.shape[0] // 8, 8, sc.shape[1]), axis=0)

    def mask_rows(sc, left):
        at = lax.broadcasted_iota(jnp.int32, sc.shape, 0)
        return jnp.where(at < left, sc, LOW)

    def y_block(p):
        return yu[p].reshape(BLOCK, D)

    def own_tile(pr, pc):
        sc = mask_cols(scores(y_block(pr), yu[pc, k]), left_y(pc) - HALF * k)
        row = lax.broadcasted_iota(jnp.int32, sc.shape, 0)
        col = lax.broadcasted_iota(jnp.int32, sc.shape, 1) + HALF * k
        col = col + jnp.where(pr == pc, 0, BLOCK)
        sc = jnp.where(row == col, LOW, sc)
        m_y[pr] = jnp.maximum(m_y[pr], fold_lanes(sc))

    def up_tile(py, pu):
        sc = scores(y_block(py), uu[pu])
        m_y[py] = jnp.maximum(m_y[py], fold_lanes(mask_cols(sc, left_u(pu))))
        c_u[pu] = jnp.maximum(c_u[pu], fold_rows(mask_rows(sc, left_y(py))))

    def down_tile(pd):
        sc = scores(y_block(3), du[pd])
        m_y[3] = jnp.maximum(m_y[3], fold_lanes(mask_cols(sc, left_d(pd))))
        c_d[pd] = jnp.maximum(c_d[pd], fold_rows(mask_rows(sc, left_y(3))))

    def cross_tile(pu, pd):
        sc = scores(uu[pu], du[pd])
        m_u[pu] = jnp.maximum(m_u[pu], fold_lanes(mask_cols(sc, left_d(pd))))
        c_d[pd] = jnp.maximum(c_d[pd], fold_rows(mask_rows(sc, left_u(pu))))

    def loop(n, body, unroll=1):
        def step(i, c):
            body(i)
            return c

        lax.fori_loop(0, n, step, 0, unroll=unroll)

    def ready_y(p):
        normalise(yraw.at[p, k], yu.at[p, k])
        recv(yraw.at[p, 1 - k], y_sem.at[p, 1 - k])
        normalise(yraw.at[p, 1 - k], yu.at[p, 1 - k])

    def ready_u(p, n_y):
        recv(uraw.at[p], u_sem.at[p])
        normalise(uraw.at[p], uu.at[p])
        loop(n_y, lambda py: up_tile(py, p), n_y)

    def ready_d(p):
        recv(draw.at[p], d_sem.at[p])
        normalise(draw.at[p], du.at[p])
        loop(p + 1, lambda pu: cross_tile(pu, p), p + 1)
        loop(p, lambda pd: cross_tile(p, pd), max(p, 1))

    m_y[...] = jnp.full(m_y.shape, LOW, F32)
    m_u[...] = jnp.full(m_u.shape, LOW, F32)
    c_u[...] = jnp.full(c_u.shape, LOW, F32)
    c_d[...] = jnp.full(c_d.shape, LOW, F32)

    loop(2, ready_y)
    loop(4, lambda i: own_tile(i // 2, i % 2), 4)
    ready_u(0, 2)
    ready_d(0)
    ready_y(2)
    loop(3, lambda p: own_tile(p, 2), 3)
    loop(2, lambda p: own_tile(2, p), 2)
    up_tile(2, 0)
    arrive(3)
    ready_u(1, 3)
    ready_d(1)
    ready_y(3)
    loop(4, lambda p: own_tile(p, 3), 4)
    loop(3, lambda p: own_tile(3, p), 3)
    loop(2, lambda p: up_tile(3, p), 2)
    ready_u(2, 4)
    ready_d(2)
    for p in range(3):
        down_tile(p)

    def flat(v):
        return jnp.max(v.T, axis=0, keepdims=True)

    s_home = x % 2
    k_home = x // 2

    def result_copies(p):
        xx = origin(p)
        return (
            remote(r_y.at[p], in_y.at[s_home, k], rs_sem.at[p, 0], iy_sem.at[s_home, k],
                   dev(z, k_home, xx, y)),
            remote(r_u.at[p], in_u.at[s_home, k], rs_sem.at[p, 1], iu_sem.at[s_home, k],
                   dev(z, k_home, xx, up)),
            remote(r_d.at[p], in_d.at[s_home, half_d], rs_sem.at[p, 2],
                   id_sem.at[s_home, half_d], dev(z, k_home, xx, down)),
        )

    for p in range(3):
        r_y[p] = flat(m_y[p])
        if p == 0:
            @pl.when(mine)
            def _():
                pltpu.make_async_copy(
                    r_y.at[0], in_y.at[s_home, k], iy_sem.at[s_home, k]
                ).start()

            @pl.when(jnp.logical_not(mine))
            def _():
                result_copies(0)[0].start()
        else:
            result_copies(p)[0].start()

    recv(uraw.at[3], u_sem.at[3])
    recv(draw.at[3], d_sem.at[3])
    normalise(uraw.at[3], uu.at[3])
    normalise(draw.at[3], du.at[3])
    up_tile(3, 3)
    all_u = scores(uu[...].reshape(4 * HALF, D), du[3])
    for p in range(4):
        sc = all_u[p * HALF : (p + 1) * HALF]
        m_u[p] = jnp.maximum(m_u[p], fold_lanes(mask_cols(sc, left_d(3))))
        c_d[3] = jnp.maximum(c_d[3], fold_rows(mask_rows(sc, left_u(p))))
    for p in range(3):
        cross_tile(3, p)
    r_y[3] = flat(m_y[3])
    result_copies(3)[0].start()
    for p in range(4):
        r_u[p] = jnp.maximum(flat(m_u[p]), jnp.max(c_u[p], axis=0, keepdims=True))
        r_d[p] = jnp.max(c_d[p], axis=0, keepdims=True)
        result_copies(p)[1].start()
        result_copies(p)[2].start()

    for s in range(2):
        for h in range(2):
            recv(in_y.at[s, h], iy_sem.at[s, h])
            recv(in_u.at[s, h], iu_sem.at[s, h])
            recv(in_d.at[s, h], id_sem.at[s, h])
        best = jnp.maximum(in_y[s, 0], in_y[s, 1])
        both = jnp.concatenate(
            [jnp.maximum(in_u[s, h], in_d[s, h]) for h in range(2)], axis=1
        )
        best = jnp.maximum(jnp.maximum(best, both), -1.0)
        at = lax.broadcasted_iota(jnp.int32, (1, BLOCK), 1) + BLOCK * m
        n = counts_ref[4 * z + 2 * k + s]
        out_ref[s : s + 1, :] = jnp.where(at < n, best, -1.0)

    @pl.when(chief)
    def _():
        remote(m_row.at[:7], m_row.at[:7], ma_sem, ma_sem, dev(z, 1 - k, x, y)).wait_send()

    @pl.when(jnp.logical_not(chief))
    def _():
        to_chief().wait_send()

    pass_on().wait_send()
    for h in range(2):
        @pl.when(here & (k != h))
        def _(h=h):
            send_own(h).wait_send()

        @pl.when(j_even != x)
        def _(h=h):
            send_far(h).wait_send()

    def finish(p):
        for copy in forwards(p):
            copy.wait_send()
        result_copies(p)[1].wait_send()
        result_copies(p)[2].wait_send()

        @pl.when((p > 0) | jnp.logical_not(mine))
        def _():
            result_copies(p)[0].wait_send()

    loop(4, finish)


def shards(embeddings, counts):
    dma = pltpu.SemaphoreType.DMA
    bf = jnp.bfloat16
    return pl.pallas_call(
        kernel,
        out_shape=jax.ShapeDtypeStruct((2, BLOCK), F32),
        in_specs=[
            pl.BlockSpec(memory_space=pl.ANY),
            pl.BlockSpec(memory_space=pl.ANY),
        ],
        out_specs=pl.BlockSpec(memory_space=pltpu.VMEM),
        scratch_shapes=[
            pltpu.SMEM((32,), jnp.int32),
            pltpu.VMEM((2, BLOCK, D), bf),
            pltpu.VMEM((HALF, D), bf),
            pltpu.VMEM((4, 2, HALF, D), bf),
            pltpu.VMEM((4, HALF, D), bf),
            pltpu.VMEM((4, HALF, D), bf),
            pltpu.VMEM((4, 2, HALF, D), bf),
            pltpu.VMEM((4, HALF, D), bf),
            pltpu.VMEM((4, HALF, D), bf),
            pltpu.VMEM((4, BLOCK, 128), F32),
            pltpu.VMEM((4, HALF, 128), F32),
            pltpu.VMEM((4, 8, HALF), F32),
            pltpu.VMEM((4, 8, HALF), F32),
            pltpu.VMEM((1, D), F32),
            pltpu.VMEM((8, 1, D), F32),
            pltpu.VMEM((4, 1, D), F32),
            pltpu.VMEM((8, 1, D), F32),
            pltpu.VMEM((1, D), F32),
            pltpu.VMEM((4, 1, BLOCK), F32),
            pltpu.VMEM((4, 1, HALF), F32),
            pltpu.VMEM((4, 1, HALF), F32),
            pltpu.VMEM((2, 2, 1, BLOCK), F32),
            pltpu.VMEM((2, 2, 1, HALF), F32),
            pltpu.VMEM((2, 2, 1, HALF), F32),
            dma((2, 2)), dma, dma, dma((4, 2)), dma((4, 3)), dma((4,)), dma((4,)),
            dma, dma, dma, dma, dma, dma, dma, dma, dma, dma,
            dma((4, 3)), dma((2, 2)), dma((2, 2)), dma((2, 2)),
        ],
        compiler_params=pltpu.CompilerParams(
            collective_id=0, has_side_effects=True, vmem_limit_bytes=64 * 1024 * 1024
        ),
        cost_estimate=pl.CostEstimate(
            flops=8 * 10**9, bytes_accessed=2 * 10**6, transcendentals=0
        ),
    )(counts, embeddings)


def solution(mesh):
    return jax.shard_map(
        shards,
        mesh=mesh,
        in_specs=(P("group", "member", None), P()),
        out_specs=P("group", "member"),
        check_vma=False,
    )
```
